128 devices in a mesh: queue: 16 (over z, y_hi, core), tensor: 8 (over x, y_lo).
Axes of the slice: x: 4, y: 4 (y_hi: 2, y_lo: 2; y = y_hi * 2 + y_lo), z: 4, core: 2. Of those that a mesh axis runs over, the one named last changes fastest.
Arguments:
- latents: bfloat16 [16, 768, 3072], P('queue'), may hold values from -6 to 6
- levels: int32 [16], P('queue'), may hold values from 0 to 49
- mod_table: bfloat16 [50, 9216], replicated, may hold values from -3 to 3
- step_size: float32 [50], replicated, may hold values from 0.2 to 1
- qkv_weight: bfloat16 [3, 3072, 3072], P(None, None, 'tensor'), may hold values from -0.109375 to 0.109375
- q_gain: float32 [128], replicated, may hold values from 0.8 to 4, as said below
- k_gain: float32 [128], replicated, may hold values from 0.8 to 4, as said below
- out_weight: bfloat16 [3072, 3072], P('tensor'), may hold values from -0.109375 to 0.109375
- fresh_noise: bfloat16 [2, 768, 3072], P(None, 'tensor'), may hold values from -6 to 6
Outputs:
- queue_out: bfloat16 [16, 768, 3072], P('queue')
The draws below stay inside these ranges and needn't reach their ends.
Inputs may be any that keep to these rules, and one draw needn't show every extreme that they name: `q_gain`: positive gains. `k_gain`: positive gains.
All inputs are finite; a program needn't handle non-finite values.
Results may differ from the reference program's by a relative error of at most 0.03.
Values may be sent and summed in bfloat16 or wider, within the bound.
A program may use at most 128 MiB of HBM per device.

```python
import math
import jax
import jax.numpy as jnp
from jax import lax

D = 3072
HEADS = 24
HD = 128
FT = 768
LEVELS = 50
STEPS = 2
FRAMES = 16
N_TENSOR = 8


def draw_q_gain(key, part):
    key = jax.random.fold_in(key, 11)
    return jax.random.uniform(key, (HD,), jnp.float32, 0.8, 2.0)


def draw_k_gain(key, part):
    key = jax.random.fold_in(key, 23)
    return jax.random.uniform(key, (HD,), jnp.float32, 0.8, 2.0)


def plant(array, key, smallest, top_value):
    index_at = [jax.random.randint(jax.random.fold_in(key, axis), (), 0, length) for axis, length in enumerate(array.shape)]
    widest = array.shape.index(max(array.shape))
    beside = index_at[:widest] + [(index_at[widest] + 1) % array.shape[widest]] + index_at[widest + 1:]
    return array.at[tuple(index_at)].set(smallest).at[tuple(beside)].set(top_value)


def block_scale(own_key, shape, split, smallest, high):
    gain = 1.0
    for position, parts in split:
        steps = jax.random.uniform(jax.random.fold_in(jax.random.fold_in(own_key, 6), position), (parts,), jnp.float32, smallest / len(split), high / len(split))
        gain = gain * jnp.repeat(jnp.exp(steps), shape[position] // parts).reshape((-1,) + (1,) * (len(shape) - 1 - position))
    return gain


def gaussian(stream_key, shape, deviation, most, shards=(), held_as=jnp.bfloat16):
    values = jax.random.normal(stream_key, shape, jnp.float32) * deviation
    if len(shards) > 0:
        values = block_scale(stream_key, shape, shards, -0.22, 0.18) * values
    return jnp.clip(values, min=-most, max=most).astype(held_as)


def setup_inputs(seed: int = 0) -> dict:
    splits = jax.random.split(jax.random.key(seed), 10)
    latents = gaussian(splits[0], (FRAMES, FT, D), 1.0, 6.0, ((0, 16),))
    levels = plant(jax.random.randint(splits[1], (FRAMES,), 0, LEVELS), jax.random.fold_in(splits[1], 1), 0, LEVELS - 1).astype(jnp.int32)
    mod_table = gaussian(splits[2], (LEVELS, 3 * D), 0.5, 3.0)
    step_size = jnp.clip(jnp.exp(jax.random.uniform(splits[3], (LEVELS,), jnp.float32, math.log(0.2), math.log(1.0))), 0.2, 1.0)
    qkv_weight = gaussian(splits[4], (3, D, HEADS * HD), D ** -0.5, 0.109375, ((2, 8),))
    q_gain = draw_q_gain(jax.random.fold_in(splits[9], 71), 0)
    k_gain = draw_k_gain(jax.random.fold_in(splits[9], 71), 0)
    out_weight = gaussian(splits[7], (HEADS * HD, D), (HEADS * HD) ** -0.5, 0.109375, ((0, 8),))
    fresh_noise = gaussian(splits[8], (STEPS, FT, D), 1.0, 6.0, ((1, 8),))
    return {"latents": latents, "levels": levels, "mod_table": mod_table, "step_size": step_size, "qkv_weight": qkv_weight, "q_gain": q_gain, "k_gain": k_gain, "out_weight": out_weight, "fresh_noise": fresh_noise}


def normalize(values, epsilon):
    return values * lax.rsqrt(lax.optimization_barrier(jnp.mean(values * values, axis=-1, keepdims=True)) + epsilon)

def reference(latents, levels, mod_table, step_size, qkv_weight, q_gain, k_gain, out_weight, fresh_noise):
    group_count = N_TENSOR
    per_group = HEADS // group_count
    onehot = (levels[:, None] == jnp.arange(LEVELS, dtype=jnp.int32)[None, :]).astype(jnp.float32)
    modulation = jnp.dot(onehot, mod_table.astype(jnp.float32), precision=lax.Precision.HIGHEST)
    rates = jnp.dot(onehot, step_size, precision=lax.Precision.HIGHEST)
    grouped_out = out_weight.reshape(group_count, per_group * HD, D).astype(jnp.float32)
    first_flags = jnp.arange(FRAMES) == 0
    queue = latents
    for step_index in range(STEPS):
        queue = jnp.concatenate([fresh_noise[step_index][None], queue[:-1]], axis=0)

        def project(items):
            frame, modrow = items
            state = frame.astype(jnp.float32)
            normed = (normalize(state, 1e-06) * (1.0 + modrow[D:2 * D]) + modrow[:D]).astype(jnp.bfloat16)
            query = jnp.dot(normed, qkv_weight[0], preferred_element_type=jnp.float32).reshape(FT, HEADS, HD)
            keys = jnp.dot(normed, qkv_weight[1], preferred_element_type=jnp.float32).reshape(FT, HEADS, HD)
            values = jnp.dot(normed, qkv_weight[2], preferred_element_type=jnp.float32).reshape(FT, HEADS, HD)
            query = (normalize(query, 1e-06) * q_gain).astype(jnp.bfloat16)
            keys = (normalize(keys, 1e-06) * k_gain).astype(jnp.bfloat16)
            return (query, keys, values.astype(jnp.bfloat16))
        query, keys, values = lax.map(project, (queue, modulation))
        prior_keys = jnp.concatenate([jnp.zeros_like(keys[:1]), keys[:-1]], axis=0)
        prior_values = jnp.concatenate([jnp.zeros_like(values[:1]), values[:-1]], axis=0)

        def attend(items):
            frame_query, frame_keys, frame_values, old_keys, old_values, is_first, modrow, rate, frame = items
            all_keys = jnp.concatenate([old_keys, frame_keys], axis=0).astype(jnp.float32)
            all_values = jnp.concatenate([old_values, frame_values], axis=0).astype(jnp.float32)
            scores = jnp.einsum('qhd,khd->hqk', frame_query.astype(jnp.float32), all_keys) / jnp.sqrt(jnp.float32(HD))
            key_valid = jnp.logical_or(jnp.arange(2 * FT) >= FT, jnp.logical_not(is_first))
            scores = jnp.where(key_valid[None, None, :], scores, jnp.float32(-1e+30))
            row_top = lax.optimization_barrier(jnp.max(scores, axis=-1, keepdims=True))
            raised = jnp.exp(scores - row_top)
            weights = (raised / lax.optimization_barrier(jnp.sum(raised, axis=-1, keepdims=True))).astype(jnp.bfloat16)
            attended = jnp.einsum('hqk,khd->qhd', weights.astype(jnp.float32), all_values).astype(jnp.bfloat16)
            attended = attended.reshape(FT, group_count, per_group * HD).astype(jnp.float32)
            partials = jnp.einsum('tgc,gcd->gtd', attended, grouped_out).astype(jnp.bfloat16)
            update = lax.optimization_barrier(jnp.sum(partials.astype(jnp.float32), axis=0))
            state = frame.astype(jnp.float32)
            return (state + rate * modrow[2 * D:] * update).astype(jnp.bfloat16)
        queue = lax.map(attend, (query, keys, values, prior_keys, prior_values, first_flags, modulation, rates, queue))
    return queue
```

```python
import functools
import math

import jax
import jax.numpy as jnp
from jax import lax
from jax.experimental import pallas as pl
from jax.experimental.pallas import tpu as pltpu
from jax.sharding import PartitionSpec as P

HD = 128
STEPS = 2
CHUNKS = 2
MESH = pl.DeviceIdType.MESH
NOISE_FROM = {1: 15, 2: 15, 3: 3, 4: 11, 5: 2, 6: 15, 7: 13}


def dot(a, b):
    return jnp.dot(a, b, preferred_element_type=jnp.float32)


def kernel(
    lat, noise, wqkv, wout, mod_own, gains, out,
    frame0, frame1, frame2, normed, wkv, wq, wo, q_buf, kv, kv_prev, mod_next,
    acc, top, total, att, att_all, own_part, part_send, part_recv, z_send,
    load_sem, send_sem, recv_sem,
):
    n_queue, n_tensor = lax.axis_size("queue"), lax.axis_size("tensor")
    n_x = n_tensor // 2
    q, t = lax.axis_index("queue"), lax.axis_index("tensor")
    x, y = t // 2, t % 2
    core = q % 2
    chunks, chunk_rows, width = frame0.shape
    rows = chunk_rows // n_tensor
    cols = wq.shape[1]
    heads = cols // HD
    half = width // 2
    last = n_queue - 1
    noise_from = {k: (v if v <= last else last) for k, v in NOISE_FROM.items()}

    def dev(queue=None, tensor=None):
        return {"queue": q if queue is None else queue, "tensor": t if tensor is None else tensor}

    def tensor_of(xx, yy):
        return lax.rem(xx + n_x, n_x) * 2 + yy

    def queue_at(d):
        return lax.rem(q + d + n_queue, n_queue)

    counter = [0]
    sent = []

    def remote(src, dst, to, keep=True):
        i = counter[0]
        counter[0] += 1
        copy = pltpu.make_async_remote_copy(
            src_ref=src, dst_ref=dst, send_sem=send_sem.at[i], recv_sem=recv_sem.at[i],
            device_id=to, device_id_type=MESH,
        )
        if keep:
            sent.append(copy)
        return copy

    def block(owner):
        return pl.ds(pl.multiple_of(owner * rows, 16), rows)

    barrier = pltpu.get_barrier_semaphore()
    partners = [dev(tensor=jnp.bitwise_xor(t, k)) for k in range(1, n_tensor)]
    steps_q = sorted({d % n_queue for d in (1, -1, 2, -2)} - {0})
    partners += [dev(queue=queue_at(d)) for d in steps_q]
    for partner in partners:
        pl.semaphore_signal(barrier, inc=1, device_id=partner, device_id_type=MESH)
    extra = {k: v for k, v in noise_from.items() if v != last}
    for k, v in extra.items():

        @pl.when(q == v)
        def _():
            pl.semaphore_signal(
                barrier, inc=1, device_id=dev(last, jnp.bitwise_xor(t, k)), device_id_type=MESH
            )

        @pl.when(q == last)
        def _():
            pl.semaphore_signal(
                barrier, inc=1, device_id=dev(v, jnp.bitwise_xor(t, k)), device_id_type=MESH
            )

    def load(src, dst, i):
        return pltpu.make_async_copy(src, dst, load_sem.at[i])

    def lat_rows(ref, owner, c):
        return ref.at[0, pl.ds(owner * rows * chunks + c * rows, rows), :]

    own_noise = [
        load(noise.at[0, pl.ds(c * rows, rows), :], frame0.at[c, block(t), :], c)
        for c in range(chunks)
    ]

    @pl.when(q != last)
    def _():
        for owner in range(n_tensor):
            load(lat_rows(lat, owner, 0), frame0.at[0, pl.ds(owner * rows, rows), :], 0).start()

    @pl.when(q == last)
    def _():
        for c in range(chunks):
            own_noise[c].start()

    load_kv = [load(wqkv.at[j + 1], wkv.at[:, pl.ds(j * cols, cols)], chunks + j) for j in range(2)]
    load_q = load(wqkv.at[0], wq, chunks + 2)
    own_wo = pl.ds(pl.multiple_of(x * cols, HD), cols)
    load_o = load(wout, wo.at[own_wo, :], chunks + 3)
    for copy in load_kv:
        copy.start()

    @pl.when(q != last)
    def _():
        for c in range(1, chunks):
            for owner in range(n_tensor):
                load(lat_rows(lat, owner, c), frame0.at[c, pl.ds(owner * rows, rows), :], c).start()

    load_q.start()
    load_o.start()

    arrivals = len(partners)
    for v in extra.values():
        arrivals = arrivals + (q == v).astype(jnp.int32) + (q == last).astype(jnp.int32)
    pl.semaphore_wait(barrier, arrivals)

    send_mod = remote(mod_own, mod_next, dev(queue=queue_at(-1)))
    send_mod.start()
    noise_copies = []
    for c in range(chunks):
        for k in range(1, n_tensor):
            copy = remote(
                noise.at[0, pl.ds(c * rows, rows), :], frame0.at[c, block(t), :],
                dev(last, jnp.bitwise_xor(t, k)), keep=False,
            )
            noise_copies.append((c, k, copy))

            @pl.when(q == noise_from[k])
            def _():
                copy.start()

    core_half = pl.ds(pl.multiple_of(core * half, HD), half)
    quarter = half // 2
    core_quarter = [
        pl.ds(pl.multiple_of(core * half + j * quarter, HD), quarter) for j in range(2)
    ]

    def wo_rows(xx):
        return pl.ds(pl.multiple_of(lax.rem(xx + n_x, n_x) * cols, HD), cols)

    wo_direct = [
        remote(wout.at[:, core_half], wo.at[own_wo, core_half], dev(tensor=tensor_of(x + d, y)))
        for d in (1, -1)
    ]
    for copy in wo_direct:
        copy.start()
    other_core = q + 1 - 2 * core
    wo_far, wo_pass = [], []

    def wo_forward():
        for i, d in enumerate((1, -1)):
            wo_direct[i].wait_recv()
            region = wo.at[wo_rows(x - d), core_quarter[i]]
            copy = remote(region, region, dev(tensor=tensor_of(x + d, y)))
            copy.start()
            wo_far.append(copy)
            region = wo.at[wo_rows(x - d), core_half]
            copy = remote(region, region, dev(queue=other_core))
            copy.start()
            wo_pass.append(copy)

    def wo_finish():
        for i in range(2):
            wo_far[i].wait_recv()
            region = wo.at[wo_rows(x + 2), core_quarter[i]]
            copy = remote(region, region, dev(queue=other_core))
            copy.start()
            wo_pass.append(copy)
        for copy in wo_pass:
            copy.wait_recv()
        load_o.wait()

    def norm_chunk(frame, mod, c):
        tile = rows

        def step(i, _):
            at = pl.ds(pl.multiple_of(i * tile, 16), tile)
            state = frame[c, at, :].astype(jnp.float32)
            scale = lax.rsqrt(jnp.mean(state * state, axis=-1, keepdims=True) + 1e-06)
            normed[c, at, :] = (state * scale * mod[1:2, :] + mod[0:1, :]).astype(jnp.bfloat16)
            return 0

        lax.fori_loop(0, chunk_rows // tile, step, 0)

    def head_norm(part, gain):
        scale = lax.rsqrt(jnp.mean(part * part, axis=-1, keepdims=True) + 1e-06)
        return (part * scale * gain).astype(jnp.bfloat16)

    def project_kv(c):
        at = pl.ds(c * chunk_rows, chunk_rows)
        both = dot(normed[c], wkv[...])
        for h in range(heads):
            lanes = slice(h * HD, (h + 1) * HD)
            kv[0, at, lanes] = head_norm(both[:, lanes], gains[1:2, :])
        kv[1, at, :] = both[:, cols:].astype(jnp.bfloat16)

    def project_q(c):
        part = dot(normed[c], wq[...])
        for h in range(heads):
            lanes = slice(h * HD, (h + 1) * HD)
            q_buf[c, :, lanes] = head_norm(part[:, lanes], gains[0:1, :])

    def send_kv(step, c):
        at = pl.ds(c * chunk_rows, chunk_rows)
        copy = remote(kv.at[:, at, :], kv_prev.at[step, :, at, :], dev(queue=queue_at(1)))
        copy.start()
        return copy

    def scores(c, lanes, keys):
        return lax.dot_general(
            q_buf[c, :, lanes], keys, (((1,), (1,)), ((), ())), preferred_element_type=jnp.float32
        )

    def attend_own(c):
        def one(h, _):
            lanes = pl.ds(pl.multiple_of(h * HD, HD), HD)
            logits = scores(c, lanes, kv[0, :, lanes])
            peak = jnp.max(logits, axis=-1, keepdims=True)
            raised = jnp.exp2(logits - peak)
            top[c, h] = jnp.broadcast_to(peak, (chunk_rows, HD))
            total[c, h] = jnp.broadcast_to(
                jnp.sum(raised, axis=-1, keepdims=True), (chunk_rows, HD)
            )
            acc[c, :, lanes] = dot(raised.astype(jnp.bfloat16), kv[1, :, lanes])
            return 0

        lax.fori_loop(0, heads, one, 0)

    def attend_prev(step, c):
        def one(h, _):
            lanes = pl.ds(pl.multiple_of(h * HD, HD), HD)
            logits = scores(c, lanes, kv_prev[step, 0, :, lanes])
            before = top[c, h]
            peak = jnp.maximum(before[:, 0:1], jnp.max(logits, axis=-1, keepdims=True))
            raised = jnp.exp2(logits - peak)
            fade = jnp.exp2(before - peak)
            weight = total[c, h] * fade + jnp.sum(raised, axis=-1, keepdims=True)
            summed = acc[c, :, lanes] * fade + dot(
                raised.astype(jnp.bfloat16), kv_prev[step, 1, :, lanes]
            )
            att[step, c, :, lanes] = (summed / weight).astype(jnp.bfloat16)
            return 0

        lax.fori_loop(0, heads, one, 0)

    def attend_alone(step, c):
        def one(h, _):
            lanes = pl.ds(pl.multiple_of(h * HD, HD), HD)
            att[step, c, :, lanes] = (acc[c, :, lanes] / total[c, h]).astype(jnp.bfloat16)
            return 0

        lax.fori_loop(0, heads, one, 0)

    def exchange_att(step, c):
        mine = pl.ds(pl.multiple_of(x * cols, HD), cols)
        copies = []
        for d in range(1, n_x):
            xx = lax.rem(x + d, n_x)
            at = pl.ds(pl.multiple_of(xx * 2 * rows, 16), 2 * rows)
            copy = remote(
                att.at[step, c, at, :], att_all.at[step, c, :, mine],
                dev(tensor=tensor_of(xx, y)),
            )
            copy.start()
            copies.append(copy)
        at = pl.ds(pl.multiple_of(x * 2 * rows, 16), 2 * rows)
        att_all[step, c, :, mine] = att[step, c, at, :]
        return copies

    n_tile = 512 if width % 512 == 0 else HD

    def project_out(step, c):
        def one(i, _):
            lanes = pl.ds(pl.multiple_of(i * n_tile, HD), n_tile)
            part = dot(att_all[step, c], wo[:, lanes])
            low, high = part[:rows], part[rows:]
            own_part[c, :, lanes] = jnp.where(y == 0, low, high)
            part_send[step, c, :, lanes] = jnp.where(y == 0, high, low).astype(jnp.bfloat16)
            return 0

        lax.fori_loop(0, width // n_tile, one, 0)
        copy = remote(
            part_send.at[step, c], part_recv.at[step, c], dev(tensor=jnp.bitwise_xor(t, 1))
        )
        copy.start()
        return copy

    def new_state(frame, mod, step, c):
        update = own_part[c] + part_recv[step, c].astype(jnp.float32)
        state = frame[c, block(t), :].astype(jnp.float32)
        return (state + mod[2:3, :] * update).astype(jnp.bfloat16)

    def ring(frame, c, owner, d, lanes):
        region = frame.at[c, block(owner), lanes]
        copy = remote(region, region, dev(tensor=tensor_of(x + d, y)))
        copy.start()
        return copy

    everything = pl.ds(0, width)
    forward_half = {1: pl.ds(0, half), -1: pl.ds(half, half)}
    partner = jnp.bitwise_xor(t, 1)

    def gather_first(frame, c):
        region = frame.at[c, block(t), :]
        across = remote(region, region, dev(tensor=partner))
        across.start()
        return {"across": across, "own": [ring(frame, c, t, d, everything) for d in (1, -1)]}

    def gather_partner(frame, c, state):
        state["across"].wait_recv()
        state["other"] = [ring(frame, c, partner, d, everything) for d in (1, -1)]

    def gather_forward(frame, c, state, which):
        copies = []
        yy = y if which == "own" else 1 - y
        for copy, d in zip(state[which], (1, -1)):
            copy.wait_recv()
            copies.append(ring(frame, c, tensor_of(x - d, yy), d, forward_half[d]))
        state["far_" + which] = copies

    def gather_wait(state):
        for which in ("far_own", "far_other"):
            for copy in state[which]:
                copy.wait_recv()

    def gather_all(frame, states):
        for c in range(chunks):
            gather_partner(frame, c, states[c])
            gather_forward(frame, c, states[c], "own")
        for c in range(chunks):
            gather_forward(frame, c, states[c], "other")

    def attention(step, position_zero, kv_copies):
        for c in range(chunks):
            attend_own(c)
        for copy in kv_copies:
            copy.wait_recv()
        exchanged = []
        for c in range(chunks):

            @pl.when(position_zero)
            def _():
                attend_alone(step, c)

            @pl.when(jnp.logical_not(position_zero))
            def _():
                attend_prev(step, c)

            exchanged.append(exchange_att(step, c))
        return exchanged

    @pl.when(q != last)
    def _():
        pltpu.make_async_copy(frame0.at[0], frame0.at[0], load_sem.at[0]).wait()

    @pl.when(q == last)
    def _():
        for c in range(chunks):
            own_noise[c].wait()
        for c, k, copy in noise_copies:
            copy.wait_recv()

    send_mod.wait_recv()
    norm_chunk(frame0, mod_next, 0)
    for copy in load_kv:
        copy.wait()
    kv_copies = []
    project_kv(0)
    kv_copies.append(send_kv(0, 0))
    for c in range(1, chunks):

        @pl.when(q != last)
        def _():
            pltpu.make_async_copy(frame0.at[c], frame0.at[c], load_sem.at[c]).wait()

        norm_chunk(frame0, mod_next, c)
        project_kv(c)
        kv_copies.append(send_kv(0, c))
    load_q.wait()
    for c in range(chunks):
        project_q(c)
    exchanged = attention(0, q == last, kv_copies)
    wo_forward()
    wo_finish()
    partials = []
    for c in range(chunks):
        for copy in exchanged[c]:
            copy.wait_recv()
        partials.append(project_out(0, c))
    shifted = []
    for c in range(chunks):
        partials[c].wait_recv()
        z_send[c] = new_state(frame0, mod_next, 0, c)
        copy = remote(z_send.at[c], frame1.at[c, block(t), :], dev(queue=queue_at(2)))
        counter[0] -= 1
        entering = remote(
            noise.at[1, pl.ds(c * rows, rows), :], frame1.at[c, block(t), :],
            dev(queue=queue_at(2)), keep=False,
        )

        @pl.when(q == last - 1)
        def _():
            entering.start()

        @pl.when(q != last - 1)
        def _():
            copy.start()

        shifted.append(copy)
    states = []
    for c in range(chunks):
        shifted[c].wait_recv()
        states.append(gather_first(frame1, c))
    gather_all(frame1, states)

    for copy in kv_copies:
        copy.wait_send()
    sent[:] = [copy for copy in sent if all(copy is not done for done in kv_copies)]
    kv_copies = []
    for c in range(chunks):
        gather_wait(states[c])
        norm_chunk(frame1, mod_own, c)
        project_kv(c)
        kv_copies.append(send_kv(1, c))
        project_q(c)
    exchanged = attention(1, q == 0, kv_copies)
    partials = []
    for c in range(chunks):
        for copy in exchanged[c]:
            copy.wait_recv()
        partials.append(project_out(1, c))
    states = []
    for c in range(chunks):
        partials[c].wait_recv()
        frame2[c, block(t), :] = new_state(frame1, mod_own, 1, c)
        states.append(gather_first(frame2, c))
    gather_all(frame2, states)
    stores = []
    for c in range(chunks):
        gather_wait(states[c])
        copy = load(frame2.at[c], out.at[c], c)
        copy.start()
        stores.append(copy)
    for copy in stores:
        copy.wait()
    for copy in sent:
        copy.wait_send()
    for c, k, copy in noise_copies:

        @pl.when(q == noise_from[k])
        def _():
            copy.wait_send()


def body(
    latents, levels, mod_table, step_size, qkv_weight, q_gain, k_gain, out_weight, fresh_noise
):
    frame_rows, width = latents.shape[1:]
    cols = qkv_weight.shape[2]
    heads = cols // HD
    n_tensor = lax.axis_size("tensor")
    chunks = CHUNKS
    chunk_rows = frame_rows // chunks
    rows = chunk_rows // n_tensor
    onehot = (jnp.arange(mod_table.shape[0], dtype=jnp.int32) == levels[0]).astype(jnp.bfloat16)
    modulation = jnp.dot(onehot[None, :], mod_table, preferred_element_type=jnp.float32)
    rate = jnp.sum(onehot.astype(jnp.float32) * step_size)
    shift, scale, gate = jnp.split(modulation, 3, axis=1)
    mod = jnp.concatenate(
        [shift, 1.0 + scale, rate * gate, jnp.zeros((5, width), jnp.float32)], axis=0
    )
    gains = jnp.concatenate(
        [
            (q_gain * (math.log2(math.e) / math.sqrt(HD)))[None],
            k_gain[None],
            jnp.zeros((6, HD), jnp.float32),
        ],
        axis=0,
    )
    bf16, f32 = jnp.bfloat16, jnp.float32
    frame = pltpu.VMEM((chunks, chunk_rows, width), bf16)
    anywhere = pl.BlockSpec(memory_space=pl.ANY)
    vmem = pl.BlockSpec(memory_space=pltpu.VMEM)
    n_copies = 128
    out = pl.pallas_call(
        kernel,
        out_shape=jax.ShapeDtypeStruct((chunks, chunk_rows, width), bf16),
        in_specs=[anywhere, anywhere, anywhere, anywhere, vmem, vmem],
        out_specs=anywhere,
        scratch_shapes=[
            frame, frame, frame, frame,
            pltpu.VMEM((width, 2 * cols), bf16),
            pltpu.VMEM((width, cols), bf16),
            pltpu.VMEM((n_tensor // 2 * cols, width), bf16),
            pltpu.VMEM((chunks, chunk_rows, cols), bf16),
            pltpu.VMEM((2, frame_rows, cols), bf16),
            pltpu.VMEM((STEPS, 2, frame_rows, cols), bf16),
            pltpu.VMEM((8, width), f32),
            pltpu.VMEM((chunks, chunk_rows, cols), f32),
            pltpu.VMEM((chunks, heads, chunk_rows, HD), f32),
            pltpu.VMEM((chunks, heads, chunk_rows, HD), f32),
            pltpu.VMEM((STEPS, chunks, chunk_rows, cols), bf16),
            pltpu.VMEM((STEPS, chunks, 2 * rows, n_tensor // 2 * cols), bf16),
            pltpu.VMEM((chunks, rows, width), f32),
            pltpu.VMEM((STEPS, chunks, rows, width), bf16),
            pltpu.VMEM((STEPS, chunks, rows, width), bf16),
            pltpu.VMEM((chunks, rows, width), bf16),
            pltpu.SemaphoreType.DMA((chunks + 4,)),
            pltpu.SemaphoreType.DMA((n_copies,)),
            pltpu.SemaphoreType.DMA((n_copies,)),
        ],
        compiler_params=pltpu.CompilerParams(
            collective_id=0, has_side_effects=True, vmem_limit_bytes=62 * 1024 * 1024
        ),
        name="denoise",
    )(latents, fresh_noise, qkv_weight, out_weight, mod, gains)
    out = out.reshape(chunks, n_tensor, rows, width).transpose(1, 0, 2, 3)
    return out.reshape(1, frame_rows, width)


def solution(mesh):
    return jax.shard_map(
        body,
        mesh=mesh,
        in_specs=(
            P("queue", None, None),
            P("queue"),
            P(),
            P(),
            P(None, None, "tensor"),
            P(),
            P(),
            P("tensor", None),
            P(None, "tensor", None),
        ),
        out_specs=P("queue", None, None),
        check_vma=False,
    )
```

```python
import functools
import math

import jax
import jax.numpy as jnp
from jax import lax
from jax.experimental import pallas as pl
from jax.experimental.pallas import tpu as pltpu
from jax.sharding import PartitionSpec as P

HD = 128
STEPS = 2
CHUNKS = 2
PARTS = 2
LAST_PART = 1536
LAST_CUT = 1280
MESH = pl.DeviceIdType.MESH
NOISE_FROM = {1: 15, 2: 15, 3: 3, 4: 11, 5: 2, 6: 15, 7: 13}


def dot(a, b):
    return jnp.dot(a, b, preferred_element_type=jnp.float32)


def kernel(
    lat, noise, wqkv, wout, mod_own, gains, out,
    frame0, frame1, frame2, normed, wkv, wq, wo, q_buf, kv, kv_prev, mod_next,
    acc, top, total, att, att_all, own_part, part_send, part_recv, z_send,
    load_sem, send_sem, recv_sem,
):
    n_queue, n_tensor = lax.axis_size("queue"), lax.axis_size("tensor")
    n_x = n_tensor // 2
    q, t = lax.axis_index("queue"), lax.axis_index("tensor")
    x, y = t // 2, t % 2
    core = q % 2
    chunks, chunk_rows, width = frame0.shape
    rows = chunk_rows // n_tensor
    cols = wq.shape[1]
    heads = cols // HD
    half = width // 2
    last = n_queue - 1
    noise_from = {k: (v if v <= last else last) for k, v in NOISE_FROM.items()}

    def dev(queue=None, tensor=None):
        return {"queue": q if queue is None else queue, "tensor": t if tensor is None else tensor}

    def tensor_of(xx, yy):
        return lax.rem(xx + n_x, n_x) * 2 + yy

    def queue_at(d):
        return lax.rem(q + d + n_queue, n_queue)

    counter = [0]
    sent = []

    def remote(src, dst, to, keep=True):
        i = counter[0]
        counter[0] += 1
        copy = pltpu.make_async_remote_copy(
            src_ref=src, dst_ref=dst, send_sem=send_sem.at[i], recv_sem=recv_sem.at[i],
            device_id=to, device_id_type=MESH,
        )
        if keep:
            sent.append(copy)
        return copy

    def block(owner):
        return pl.ds(pl.multiple_of(owner * rows, 16), rows)

    barrier = pltpu.get_barrier_semaphore()
    partners = [dev(tensor=jnp.bitwise_xor(t, k)) for k in range(1, n_tensor)]
    partners += [dev(queue=queue_at(d)) for d in sorted({1, n_queue - 1})]
    partners += [dev(queue_at(d), jnp.bitwise_xor(t, 1)) for d in sorted({2, n_queue - 2})]
    for to in partners:
        pl.semaphore_signal(barrier, inc=1, device_id=to, device_id_type=MESH)
    extra = {k: v for k, v in noise_from.items() if v != last}
    for k, v in extra.items():

        @pl.when(q == v)
        def _():
            pl.semaphore_signal(
                barrier, inc=1, device_id=dev(last, jnp.bitwise_xor(t, k)), device_id_type=MESH
            )

        @pl.when(q == last)
        def _():
            pl.semaphore_signal(
                barrier, inc=1, device_id=dev(v, jnp.bitwise_xor(t, k)), device_id_type=MESH
            )

    def load(src, dst, i):
        return pltpu.make_async_copy(src, dst, load_sem.at[i])

    def lat_rows(ref, owner, c):
        return ref.at[0, pl.ds(owner * rows * chunks + c * rows, rows), :]

    own_noise = [
        load(noise.at[0, pl.ds(c * rows, rows), :], frame0.at[c, block(t), :], c)
        for c in range(chunks)
    ]

    @pl.when(q != last)
    def _():
        for owner in range(n_tensor):
            load(lat_rows(lat, owner, 0), frame0.at[0, pl.ds(owner * rows, rows), :], 0).start()

    @pl.when(q == last)
    def _():
        for c in range(chunks):
            own_noise[c].start()

    load_kv = [load(wqkv.at[j + 1], wkv.at[:, pl.ds(j * cols, cols)], chunks + j) for j in range(2)]
    load_q = load(wqkv.at[0], wq, chunks + 2)
    own_wo = pl.ds(pl.multiple_of(x * cols, HD), cols)
    load_o = load(wout, wo.at[own_wo, :], chunks + 3)
    for copy in load_kv:
        copy.start()

    @pl.when(q != last)
    def _():
        for c in range(1, chunks):
            for owner in range(n_tensor):
                load(lat_rows(lat, owner, c), frame0.at[c, pl.ds(owner * rows, rows), :], c).start()

    load_q.start()
    load_o.start()

    arrivals = len(partners)
    for v in extra.values():
        arrivals = arrivals + (q == v).astype(jnp.int32) + (q == last).astype(jnp.int32)
    pl.semaphore_wait(barrier, arrivals)

    send_mod = remote(mod_own, mod_next, dev(queue=queue_at(-1)))
    send_mod.start()
    noise_copies = []
    for c in range(chunks):
        for k in range(1, n_tensor):
            copy = remote(
                noise.at[0, pl.ds(c * rows, rows), :], frame0.at[c, block(t), :],
                dev(last, jnp.bitwise_xor(t, k)), keep=False,
            )
            noise_copies.append((c, k, copy))

            @pl.when(q == noise_from[k])
            def _():
                copy.start()

    core_half = pl.ds(pl.multiple_of(core * half, HD), half)
    quarter = half // 2
    core_quarter = [
        pl.ds(pl.multiple_of(core * half + j * quarter, HD), quarter) for j in range(2)
    ]

    def wo_rows(xx):
        return pl.ds(pl.multiple_of(lax.rem(xx + n_x, n_x) * cols, HD), cols)

    wo_direct = [
        remote(wout.at[:, core_half], wo.at[own_wo, core_half], dev(tensor=tensor_of(x + d, y)))
        for d in (1, -1)
    ]
    for copy in wo_direct:
        copy.start()
    other_core = q + 1 - 2 * core
    wo_far, wo_pass = [], []

    def wo_forward():
        for i, d in enumerate((1, -1)):
            wo_direct[i].wait_recv()
            region = wo.at[wo_rows(x - d), core_quarter[i]]
            copy = remote(region, region, dev(tensor=tensor_of(x + d, y)))
            copy.start()
            wo_far.append(copy)
            region = wo.at[wo_rows(x - d), core_half]
            copy = remote(region, region, dev(queue=other_core))
            copy.start()
            wo_pass.append(copy)

    def wo_finish():
        for i in range(2):
            wo_far[i].wait_recv()
            region = wo.at[wo_rows(x + 2), core_quarter[i]]
            copy = remote(region, region, dev(queue=other_core))
            copy.start()
            wo_pass.append(copy)
        for copy in wo_pass:
            copy.wait_recv()
        load_o.wait()

    def norm_chunk(frame, mod, c):
        tile = rows

        def step(i, _):
            at = pl.ds(pl.multiple_of(i * tile, 16), tile)
            state = frame[c, at, :].astype(jnp.float32)
            scale = lax.rsqrt(jnp.mean(state * state, axis=-1, keepdims=True) + 1e-06)
            normed[c, at, :] = (state * scale * mod[1:2, :] + mod[0:1, :]).astype(jnp.bfloat16)
            return 0

        lax.fori_loop(0, chunk_rows // tile, step, 0)

    def head_norm(part, gain):
        scale = lax.rsqrt(jnp.mean(part * part, axis=-1, keepdims=True) + 1e-06)
        return (part * scale * gain).astype(jnp.bfloat16)

    def project_kv(c):
        at = pl.ds(c * chunk_rows, chunk_rows)
        both = dot(normed[c], wkv[...])
        for h in range(heads):
            lanes = slice(h * HD, (h + 1) * HD)
            kv[0, at, lanes] = head_norm(both[:, lanes], gains[1:2, :])
        kv[1, at, :] = both[:, cols:].astype(jnp.bfloat16)

    def project_q(c):
        part = dot(normed[c], wq[...])
        for h in range(heads):
            lanes = slice(h * HD, (h + 1) * HD)
            q_buf[c, :, lanes] = head_norm(part[:, lanes], gains[0:1, :])

    def send_kv(step, c):
        at = pl.ds(c * chunk_rows, chunk_rows)
        copy = remote(kv.at[:, at, :], kv_prev.at[step, :, at, :], dev(queue=queue_at(1)))
        copy.start()
        return copy

    def scores(c, lanes, keys):
        return lax.dot_general(
            q_buf[c, :, lanes], keys, (((1,), (1,)), ((), ())), preferred_element_type=jnp.float32
        )

    def attend_own(c):
        def one(h, _):
            lanes = pl.ds(pl.multiple_of(h * HD, HD), HD)
            logits = scores(c, lanes, kv[0, :, lanes])
            peak = jnp.max(logits, axis=-1, keepdims=True)
            raised = jnp.exp2(logits - peak)
            top[c, h] = jnp.broadcast_to(peak, (chunk_rows, HD))
            total[c, h] = jnp.broadcast_to(
                jnp.sum(raised, axis=-1, keepdims=True), (chunk_rows, HD)
            )
            acc[c, :, lanes] = dot(raised.astype(jnp.bfloat16), kv[1, :, lanes])
            return 0

        lax.fori_loop(0, heads, one, 0)

    def attend_prev(step, c):
        def one(h, _):
            lanes = pl.ds(pl.multiple_of(h * HD, HD), HD)
            logits = scores(c, lanes, kv_prev[step, 0, :, lanes])
            before = top[c, h]
            peak = jnp.maximum(before[:, 0:1], jnp.max(logits, axis=-1, keepdims=True))
            raised = jnp.exp2(logits - peak)
            fade = jnp.exp2(before - peak)
            weight = total[c, h] * fade + jnp.sum(raised, axis=-1, keepdims=True)
            summed = acc[c, :, lanes] * fade + dot(
                raised.astype(jnp.bfloat16), kv_prev[step, 1, :, lanes]
            )
            att[step, c, :, lanes] = (summed / weight).astype(jnp.bfloat16)
            return 0

        lax.fori_loop(0, heads, one, 0)

    def attend_alone(step, c):
        def one(h, _):
            lanes = pl.ds(pl.multiple_of(h * HD, HD), HD)
            att[step, c, :, lanes] = (acc[c, :, lanes] / total[c, h]).astype(jnp.bfloat16)
            return 0

        lax.fori_loop(0, heads, one, 0)

    def exchange_att(step, c):
        mine = pl.ds(pl.multiple_of(x * cols, HD), cols)
        copies = []
        for d in range(1, n_x):
            xx = lax.rem(x + d, n_x)
            at = pl.ds(pl.multiple_of(xx * 2 * rows, 16), 2 * rows)
            copy = remote(
                att.at[step, c, at, :], att_all.at[step, c, :, mine],
                dev(tensor=tensor_of(xx, y)),
            )
            copy.start()
            copies.append(copy)
        at = pl.ds(pl.multiple_of(x * 2 * rows, 16), 2 * rows)
        att_all[step, c, :, mine] = att[step, c, at, :]
        return copies

    parts = PARTS
    part_cols = width // parts
    n_tile = 512 if part_cols % 512 == 0 else HD
    units = [(c, k) for c in range(chunks) for k in range(parts)]

    def project_out(step, c, k):
        def one(i, _):
            lanes = pl.ds(pl.multiple_of(k * part_cols + i * n_tile, HD), n_tile)
            part = dot(att_all[step, c], wo[:, lanes])
            low, high = part[:rows], part[rows:]
            own_part[c, :, lanes] = jnp.where(y == 0, low, high)
            part_send[step, c, :, lanes] = jnp.where(y == 0, high, low).astype(jnp.bfloat16)
            return 0

        lax.fori_loop(0, part_cols // n_tile, one, 0)
        lanes = pl.ds(k * part_cols, part_cols)
        copy = remote(
            part_send.at[step, c, :, lanes], part_recv.at[step, c, :, lanes], dev(tensor=partner)
        )
        copy.start()
        return copy

    def new_state(frame, mod, step, c, k):
        lanes = pl.ds(k * part_cols, part_cols)
        update = own_part[c, :, lanes] + part_recv[step, c, :, lanes].astype(jnp.float32)
        state = frame[c, block(t), lanes].astype(jnp.float32)
        return (state + mod[2:3, lanes] * update).astype(jnp.bfloat16)

    def move(frame, c, owner, lanes, to):
        region = frame.at[c, block(owner), lanes]
        copy = remote(region, region, to)
        copy.start()
        return copy

    partner = jnp.bitwise_xor(t, 1)
    WAYS = (1, -1)

    class Gather:
        def __init__(self, frame, c, k, side, cut):
            self.frame, self.c, self.side = frame, c, side
            self.start = k * part_cols
            self.cut = cut

        def cols(self, low, high):
            return pl.ds(self.start + low, high - low)

        def ring(self, owner_x, side, d, low, high):
            owner = tensor_of(owner_x, side)
            return move(self.frame, self.c, owner, self.cols(low, high), dev(tensor=tensor_of(x + d, y)))

        def cross(self, owner_x, low):
            owner = tensor_of(owner_x, self.side)
            return move(self.frame, self.c, owner, self.cols(low, part_cols), dev(tensor=partner))

        def first(self):
            self.across = self.cross(x, 0)
            self.own = [self.ring(x, self.side, d, 0, part_cols) for d in WAYS]

        def second(self):
            self.across.wait_recv()
            self.other = [self.ring(x, 1 - self.side, d, 0, self.cut) for d in WAYS]

        def forward_own(self):
            mid = part_cols // 2
            self.far, self.crossed = [], []
            for copy, d in zip(self.own, WAYS):
                copy.wait_recv()
                low, high = (0, mid) if d == 1 else (mid, part_cols)
                self.far.append(self.ring(x - d, self.side, d, low, high))
                if self.cut < part_cols:
                    self.crossed.append(self.cross(x - d, self.cut))

        def forward_other(self):
            mid = self.cut // 2
            self.far_other = []
            for copy, d in zip(self.other, WAYS):
                copy.wait_recv()
                low, high = (0, mid) if d == 1 else (mid, self.cut)
                self.far_other.append(self.ring(x - d, 1 - self.side, d, low, high))
            if self.cut < part_cols:
                self.far[1].wait_recv()
                self.crossed.append(self.cross(x + 2, self.cut))

        def wait(self):
            self.far[0].wait_recv()
            if self.cut == part_cols:
                self.far[1].wait_recv()
            for copy in self.far_other + self.crossed:
                copy.wait_recv()

    def output_projection(step, exchanged):
        partials = []
        for c in range(chunks):
            for copy in exchanged[c]:
                copy.wait_recv()
            for k in range(parts):
                partials.append(project_out(step, c, k))
        return partials

    def attention(step, position_zero, kv_copies):
        for c in range(chunks):
            attend_own(c)
        for copy in kv_copies:
            copy.wait_recv()
        exchanged = []
        for c in range(chunks):

            @pl.when(position_zero)
            def _():
                attend_alone(step, c)

            @pl.when(jnp.logical_not(position_zero))
            def _():
                attend_prev(step, c)

            exchanged.append(exchange_att(step, c))
        return exchanged

    @pl.when(q != last)
    def _():
        pltpu.make_async_copy(frame0.at[0], frame0.at[0], load_sem.at[0]).wait()

    @pl.when(q == last)
    def _():
        for c in range(chunks):
            own_noise[c].wait()
        for c, k, copy in noise_copies:
            copy.wait_recv()

    send_mod.wait_recv()
    norm_chunk(frame0, mod_next, 0)
    for copy in load_kv:
        copy.wait()
    kv_copies = []
    project_kv(0)
    kv_copies.append(send_kv(0, 0))
    for c in range(1, chunks):

        @pl.when(q != last)
        def _():
            pltpu.make_async_copy(frame0.at[c], frame0.at[c], load_sem.at[c]).wait()

        norm_chunk(frame0, mod_next, c)
        project_kv(c)
        kv_copies.append(send_kv(0, c))
    load_q.wait()
    for c in range(chunks):
        project_q(c)
    exchanged = attention(0, q == last, kv_copies)
    wo_forward()
    wo_finish()
    partials = output_projection(0, exchanged)

    def send_shifted(u):
        c, k = units[u]
        lanes = pl.ds(k * part_cols, part_cols)
        partials[u].wait_recv()
        z_send[c, :, lanes] = new_state(frame0, mod_next, 0, c, k)
        place = frame1.at[c, block(t), lanes]
        to = dev(queue_at(2), partner)
        copy = remote(z_send.at[c, :, lanes], place, to)
        counter[0] -= 1
        entering = remote(noise.at[1, pl.ds(c * rows, rows), lanes], place, to, keep=False)

        @pl.when(q == last - 1)
        def _():
            entering.start()

        @pl.when(q != last - 1)
        def _():
            copy.start()

        return copy

    n_units = len(units)
    shifted = [None] * n_units
    gathers = [Gather(frame1, c, k, 1 - y, part_cols) for c, k in units]

    def first_after_shift(u):
        shifted[u].wait_recv()
        gathers[u].first()

    for tick in range(n_units + 3):
        if tick < n_units:
            shifted[tick] = send_shifted(tick)
        if 0 <= tick - 1 < n_units:
            first_after_shift(tick - 1)
        if 0 <= tick - 2 < n_units:
            gathers[tick - 2].second()
            gathers[tick - 2].forward_own()
        if 0 <= tick - 3 < n_units - parts:
            gathers[tick - 3].forward_other()

    for copy in kv_copies:
        copy.wait_send()
    sent[:] = [copy for copy in sent if all(copy is not done for done in kv_copies)]
    kv_copies = []
    for c in range(chunks):
        for k in range(parts):
            gathers[c * parts + k].wait()
        norm_chunk(frame1, mod_own, c)
        project_kv(c)
        kv_copies.append(send_kv(1, c))
        if c == chunks - 2:
            for u in range(n_units - parts, n_units):
                gathers[u].forward_other()
        project_q(c)
    exchanged = attention(1, q == 0, kv_copies)
    partials = output_projection(1, exchanged)
    cut = LAST_CUT if part_cols == LAST_PART else part_cols // 2
    gathers = [Gather(frame2, c, k, y, cut) for c, k in units]
    stores = []

    def store(c):
        for k in range(parts):
            gathers[c * parts + k].wait()
        copy = load(frame2.at[c], out.at[c], c)
        copy.start()
        stores.append(copy)

    for tick in range(n_units + 2):
        if tick < n_units:
            c, k = units[tick]
            partials[tick].wait_recv()
            frame2[c, block(t), pl.ds(k * part_cols, part_cols)] = new_state(
                frame1, mod_own, 1, c, k
            )
            gathers[tick].first()
        if 0 <= tick - 1 < n_units:
            gathers[tick - 1].second()
            gathers[tick - 1].forward_own()
        if 0 <= tick - 2 < n_units:
            gathers[tick - 2].forward_other()
    for c in range(chunks):
        store(c)
    for copy in stores:
        copy.wait()
    for copy in sent:
        copy.wait_send()
    for c, k, copy in noise_copies:

        @pl.when(q == noise_from[k])
        def _():
            copy.wait_send()


def body(
    latents, levels, mod_table, step_size, qkv_weight, q_gain, k_gain, out_weight, fresh_noise
):
    frame_rows, width = latents.shape[1:]
    cols = qkv_weight.shape[2]
    heads = cols // HD
    n_tensor = lax.axis_size("tensor")
    chunks = CHUNKS
    chunk_rows = frame_rows // chunks
    rows = chunk_rows // n_tensor
    onehot = (jnp.arange(mod_table.shape[0], dtype=jnp.int32) == levels[0]).astype(jnp.bfloat16)
    modulation = jnp.dot(onehot[None, :], mod_table, preferred_element_type=jnp.float32)
    rate = jnp.sum(onehot.astype(jnp.float32) * step_size)
    shift, scale, gate = jnp.split(modulation, 3, axis=1)
    mod = jnp.concatenate(
        [shift, 1.0 + scale, rate * gate, jnp.zeros((5, width), jnp.float32)], axis=0
    )
    gains = jnp.concatenate(
        [
            (q_gain * (math.log2(math.e) / math.sqrt(HD)))[None],
            k_gain[None],
            jnp.zeros((6, HD), jnp.float32),
        ],
        axis=0,
    )
    bf16, f32 = jnp.bfloat16, jnp.float32
    frame = pltpu.VMEM((chunks, chunk_rows, width), bf16)
    anywhere = pl.BlockSpec(memory_space=pl.ANY)
    vmem = pl.BlockSpec(memory_space=pltpu.VMEM)
    n_copies = 192
    out = pl.pallas_call(
        kernel,
        out_shape=jax.ShapeDtypeStruct((chunks, chunk_rows, width), bf16),
        in_specs=[anywhere, anywhere, anywhere, anywhere, vmem, vmem],
        out_specs=anywhere,
        scratch_shapes=[
            frame, frame, frame, frame,
            pltpu.VMEM((width, 2 * cols), bf16),
            pltpu.VMEM((width, cols), bf16),
            pltpu.VMEM((n_tensor // 2 * cols, width), bf16),
            pltpu.VMEM((chunks, chunk_rows, cols), bf16),
            pltpu.VMEM((2, frame_rows, cols), bf16),
            pltpu.VMEM((STEPS, 2, frame_rows, cols), bf16),
            pltpu.VMEM((8, width), f32),
            pltpu.VMEM((chunks, chunk_rows, cols), f32),
            pltpu.VMEM((chunks, heads, chunk_rows, HD), f32),
            pltpu.VMEM((chunks, heads, chunk_rows, HD), f32),
            pltpu.VMEM((STEPS, chunks, chunk_rows, cols), bf16),
            pltpu.VMEM((STEPS, chunks, 2 * rows, n_tensor // 2 * cols), bf16),
            pltpu.VMEM((chunks, rows, width), f32),
            pltpu.VMEM((STEPS, chunks, rows, width), bf16),
            pltpu.VMEM((STEPS, chunks, rows, width), bf16),
            pltpu.VMEM((chunks, rows, width), bf16),
            pltpu.SemaphoreType.DMA((chunks + 4,)),
            pltpu.SemaphoreType.DMA((n_copies,)),
            pltpu.SemaphoreType.DMA((n_copies,)),
        ],
        compiler_params=pltpu.CompilerParams(
            collective_id=0, has_side_effects=True, vmem_limit_bytes=62 * 1024 * 1024
        ),
        name="denoise",
    )(latents, fresh_noise, qkv_weight, out_weight, mod, gains)
    out = out.reshape(chunks, n_tensor, rows, width).transpose(1, 0, 2, 3)
    return out.reshape(1, frame_rows, width)


def solution(mesh):
    return jax.shard_map(
        body,
        mesh=mesh,
        in_specs=(
            P("queue", None, None),
            P("queue"),
            P(),
            P(),
            P(None, None, "tensor"),
            P(),
            P(),
            P("tensor", None),
            P(None, "tensor", None),
        ),
        out_specs=P("queue", None, None),
        check_vma=False,
    )
```

```python
import functools
import math

import jax
import jax.numpy as jnp
from jax import lax
from jax.experimental import pallas as pl
from jax.experimental.pallas import tpu as pltpu
from jax.sharding import PartitionSpec as P

HD = 128
STEPS = 2
CHUNKS = 2
PARTS = 2
LAST_PART = 1536
LAST_CUT = 1280
MESH = pl.DeviceIdType.MESH
NOISE_FROM = {1: (15, 15), 2: (15, 15), 3: (3, 3), 4: (11, 11), 5: (2, 10), 6: (15, 15), 7: (13, 13)}


def dot(a, b):
    return jnp.dot(a, b, preferred_element_type=jnp.float32)


def kernel(
    levels, lat, noise, wqkv, wout, mod_table, step_size, q_gain, k_gain, out,
    frame0, frame1, frame2, normed, wkv, wq, wo, q_buf, kv, kv_prev, mod_own, mod_next, gains,
    acc, top, total, att, att_all, own_part, part_send, part_recv, z_send,
    load_sem, send_sem, recv_sem,
):
    n_queue, n_tensor = lax.axis_size("queue"), lax.axis_size("tensor")
    n_x = n_tensor // 2
    q, t = lax.axis_index("queue"), lax.axis_index("tensor")
    x, y = t // 2, t % 2
    core = q % 2
    chunks, chunk_rows, width = frame0.shape
    rows = chunk_rows // n_tensor
    cols = wq.shape[1]
    heads = cols // HD
    half = width // 2
    last = n_queue - 1
    noise_from = {
        (k, c): (v[c % 2] if v[c % 2] <= last else last)
        for k, v in NOISE_FROM.items()
        for c in range(chunks)
    }

    def dev(queue=None, tensor=None):
        return {"queue": q if queue is None else queue, "tensor": t if tensor is None else tensor}

    def tensor_of(xx, yy):
        return lax.rem(xx + n_x, n_x) * 2 + yy

    def queue_at(d):
        return lax.rem(q + d + n_queue, n_queue)

    counter = [0]
    sent = []

    def remote(src, dst, to, keep=True):
        i = counter[0]
        counter[0] += 1
        copy = pltpu.make_async_remote_copy(
            src_ref=src, dst_ref=dst, send_sem=send_sem.at[i], recv_sem=recv_sem.at[i],
            device_id=to, device_id_type=MESH,
        )
        if keep:
            sent.append(copy)
        return copy

    def block(owner):
        return pl.ds(pl.multiple_of(owner * rows, 16), rows)

    barrier = pltpu.get_barrier_semaphore()
    partners = [dev(tensor=jnp.bitwise_xor(t, k)) for k in range(1, n_tensor)]
    near = {1, n_queue - 1} | ({4, n_queue - 4} if n_queue > 4 else set())
    partners += [dev(queue=queue_at(d)) for d in sorted(near)]
    partners += [dev(queue_at(d), jnp.bitwise_xor(t, 1)) for d in sorted({2, n_queue - 2})]
    for to in partners:
        pl.semaphore_signal(barrier, inc=1, device_id=to, device_id_type=MESH)
    extra = sorted({(k, v) for (k, _), v in noise_from.items() if v != last})
    for k, v in extra:

        @pl.when(q == v)
        def _():
            pl.semaphore_signal(
                barrier, inc=1, device_id=dev(last, jnp.bitwise_xor(t, k)), device_id_type=MESH
            )

        @pl.when(q == last)
        def _():
            pl.semaphore_signal(
                barrier, inc=1, device_id=dev(v, jnp.bitwise_xor(t, k)), device_id_type=MESH
            )

    def load(src, dst, i):
        return pltpu.make_async_copy(src, dst, load_sem.at[i])

    def lat_rows(ref, owner, c):
        return ref.at[0, pl.ds(owner * rows * chunks + c * rows, rows), :]

    own_noise = [
        load(noise.at[0, pl.ds(c * rows, rows), :], frame0.at[c, block(t), :], c)
        for c in range(chunks)
    ]

    @pl.when(q != last)
    def _():
        for owner in range(n_tensor):
            load(lat_rows(lat, owner, 0), frame0.at[0, pl.ds(owner * rows, rows), :], 0).start()

    @pl.when(q == last)
    def _():
        for c in range(chunks):
            own_noise[c].start()

    load_kv = [load(wqkv.at[j + 1], wkv.at[:, pl.ds(j * cols, cols)], chunks + j) for j in range(2)]
    load_q = load(wqkv.at[0], wq, chunks + 2)
    own_wo = pl.ds(pl.multiple_of(x * cols, HD), cols)
    load_o = load(wout, wo.at[own_wo, :], chunks + 3)
    for copy in load_kv:
        copy.start()

    @pl.when(q != last)
    def _():
        for c in range(1, chunks):
            for owner in range(n_tensor):
                load(lat_rows(lat, owner, c), frame0.at[c, pl.ds(owner * rows, rows), :], c).start()

    load_q.start()
    load_o.start()

    n_levels = mod_table.shape[0]
    hot = lax.broadcasted_iota(jnp.int32, (8, n_levels), 1) == levels[0]
    rate = jnp.sum(jnp.where(hot, step_size[...], 0.0), axis=1, keepdims=True)[0:1]
    hot = hot.astype(jnp.float32).astype(jnp.bfloat16)
    mod_own[...] = jnp.zeros_like(mod_own)
    mod_own[0:1, :] = dot(hot, mod_table[:, :width])[0:1]
    mod_own[1:2, :] = 1.0 + dot(hot, mod_table[:, width : 2 * width])[0:1]
    mod_own[2:3, :] = rate * dot(hot, mod_table[:, 2 * width :])[0:1]
    gains[0:1, :] = q_gain[...] * (math.log2(math.e) / math.sqrt(HD))
    gains[1:2, :] = k_gain[...]

    arrivals = len(partners)
    for _, v in extra:
        arrivals = arrivals + (q == v).astype(jnp.int32) + (q == last).astype(jnp.int32)
    pl.semaphore_wait(barrier, arrivals)

    send_mod = remote(mod_own, mod_next, dev(queue=queue_at(-1)))
    send_mod.start()
    noise_copies = []
    for c in range(chunks):
        for k in range(1, n_tensor):
            copy = remote(
                noise.at[0, pl.ds(c * rows, rows), :], frame0.at[c, block(t), :],
                dev(last, jnp.bitwise_xor(t, k)), keep=False,
            )
            noise_copies.append((c, k, copy))

            @pl.when(q == noise_from[k, c])
            def _():
                copy.start()

    n_z = n_queue // 4
    z_side = (q // 4) % 2 if n_z > 1 else 0
    sides = 2 if n_z > 1 else 1
    share = width // (2 * sides)

    def share_cols(side, part=None):
        start = (side * 2 + core) * share
        if part is None:
            return pl.ds(pl.multiple_of(start, HD), share)
        return pl.ds(pl.multiple_of(start + part * (share // 2), HD), share // 2)

    def wo_region(xx, side, part=None, row_part=None):
        start, size = lax.rem(xx + n_x, n_x) * cols, cols
        if row_part is not None:
            start, size = start + row_part * (cols // 2), cols // 2
        return wo.at[pl.ds(pl.multiple_of(start, 16), size), share_cols(side, part)]

    other_core = q + 1 - 2 * core
    z_ways = (4, -4)
    wo_direct, wo_far, wo_pass, wo_z = [], [], [], []

    def wo_move(region, to, into):
        copy = remote(region, region, to)
        copy.start()
        into.append(copy)

    def wo_start():
        for d in (1, -1):
            copy = remote(
                wout.at[:, share_cols(z_side)], wo.at[own_wo, share_cols(z_side)],
                dev(tensor=tensor_of(x + d, y)),
            )
            copy.start()
            wo_direct.append(copy)

    def wo_forward():
        for i, d in enumerate((1, -1)):
            wo_direct[i].wait_recv()
            wo_move(wo_region(x - d, z_side, part=i), dev(tensor=tensor_of(x + d, y)), wo_far)
            if sides == 2:
                for e, dz in enumerate(z_ways):
                    wo_move(wo_region(x - d, z_side, row_part=e), dev(queue=queue_at(dz)), wo_z)
            wo_move(wo_region(x - d, z_side), dev(queue=other_core), wo_pass)

    def wo_forward_far():
        for i in range(2):
            wo_far[i].wait_recv()
            if sides == 2:
                wo_move(wo_region(x + 2, z_side, part=i), dev(queue=queue_at(z_ways[i])), wo_z)
        wo_move(wo_region(x + 2, z_side), dev(queue=other_core), wo_pass)

    def wo_other_side():
        if sides == 2:
            for i, xx in enumerate((x - 1, x + 1, x + 2)):
                for e in range(2):
                    wo_z[2 * i + e].wait_recv()
                wo_move(wo_region(xx, 1 - z_side), dev(queue=other_core), wo_pass)

    def wo_finish():
        for copy in wo_pass:
            copy.wait_recv()
        load_o.wait()

    def norm_chunk(frame, mod, c):
        tile = rows

        def step(i, _):
            at = pl.ds(pl.multiple_of(i * tile, 16), tile)
            state = frame[c, at, :].astype(jnp.float32)
            scale = lax.rsqrt(jnp.mean(state * state, axis=-1, keepdims=True) + 1e-06)
            normed[c, at, :] = (state * scale * mod[1:2, :] + mod[0:1, :]).astype(jnp.bfloat16)
            return 0

        lax.fori_loop(0, chunk_rows // tile, step, 0)

    def head_norm(part, gain):
        scale = lax.rsqrt(jnp.mean(part * part, axis=-1, keepdims=True) + 1e-06)
        return (part * scale * gain).astype(jnp.bfloat16)

    def project_kv(c):
        at = pl.ds(c * chunk_rows, chunk_rows)
        both = dot(normed[c], wkv[...])
        for h in range(heads):
            lanes = slice(h * HD, (h + 1) * HD)
            kv[0, at, lanes] = head_norm(both[:, lanes], gains[1:2, :])
        kv[1, at, :] = both[:, cols:].astype(jnp.bfloat16)

    def project_q(c):
        part = dot(normed[c], wq[...])
        for h in range(heads):
            lanes = slice(h * HD, (h + 1) * HD)
            q_buf[c, :, lanes] = head_norm(part[:, lanes], gains[0:1, :])

    def send_kv(step, c):
        at = pl.ds(c * chunk_rows, chunk_rows)
        copy = remote(kv.at[:, at, :], kv_prev.at[step, :, at, :], dev(queue=queue_at(1)))
        copy.start()
        return copy

    def scores(c, lanes, keys):
        return lax.dot_general(
            q_buf[c, :, lanes], keys, (((1,), (1,)), ((), ())), preferred_element_type=jnp.float32
        )

    def attend_own(c):
        def one(h, _):
            lanes = pl.ds(pl.multiple_of(h * HD, HD), HD)
            logits = scores(c, lanes, kv[0, :, lanes])
            peak = jnp.max(logits, axis=-1, keepdims=True)
            raised = jnp.exp2(logits - peak)
            top[c, h] = jnp.broadcast_to(peak, (chunk_rows, HD))
            total[c, h] = jnp.broadcast_to(
                jnp.sum(raised, axis=-1, keepdims=True), (chunk_rows, HD)
            )
            acc[c, :, lanes] = dot(raised.astype(jnp.bfloat16), kv[1, :, lanes])
            return 0

        lax.fori_loop(0, heads, one, 0)

    def attend_prev(step, c):
        def one(h, _):
            lanes = pl.ds(pl.multiple_of(h * HD, HD), HD)
            logits = scores(c, lanes, kv_prev[step, 0, :, lanes])
            before = top[c, h]
            peak = jnp.maximum(before[:, 0:1], jnp.max(logits, axis=-1, keepdims=True))
            raised = jnp.exp2(logits - peak)
            fade = jnp.exp2(before - peak)
            weight = total[c, h] * fade + jnp.sum(raised, axis=-1, keepdims=True)
            summed = acc[c, :, lanes] * fade + dot(
                raised.astype(jnp.bfloat16), kv_prev[step, 1, :, lanes]
            )
            att[step, c, :, lanes] = (summed / weight).astype(jnp.bfloat16)
            return 0

        lax.fori_loop(0, heads, one, 0)

    def attend_alone(step, c):
        def one(h, _):
            lanes = pl.ds(pl.multiple_of(h * HD, HD), HD)
            att[step, c, :, lanes] = (acc[c, :, lanes] / total[c, h]).astype(jnp.bfloat16)
            return 0

        lax.fori_loop(0, heads, one, 0)

    def exchange_att(step, c):
        mine = pl.ds(pl.multiple_of(x * cols, HD), cols)
        copies = []
        for d in range(1, n_x):
            xx = lax.rem(x + d, n_x)
            at = pl.ds(pl.multiple_of(xx * 2 * rows, 16), 2 * rows)
            copy = remote(
                att.at[step, c, at, :], att_all.at[step, c, :, mine],
                dev(tensor=tensor_of(xx, y)),
            )
            copy.start()
            copies.append(copy)
        at = pl.ds(pl.multiple_of(x * 2 * rows, 16), 2 * rows)
        att_all[step, c, :, mine] = att[step, c, at, :]
        return copies

    parts = PARTS
    part_cols = width // parts
    n_tile = 512 if part_cols % 512 == 0 else HD
    units = [(c, k) for c in range(chunks) for k in range(parts)]

    def project_out(step, c, k):
        def one(i, _):
            lanes = pl.ds(pl.multiple_of(k * part_cols + i * n_tile, HD), n_tile)
            part = dot(att_all[step, c], wo[:, lanes])
            low, high = part[:rows], part[rows:]
            own_part[c, :, lanes] = jnp.where(y == 0, low, high)
            part_send[step, c, :, lanes] = jnp.where(y == 0, high, low).astype(jnp.bfloat16)
            return 0

        lax.fori_loop(0, part_cols // n_tile, one, 0)
        lanes = pl.ds(k * part_cols, part_cols)
        copy = remote(
            part_send.at[step, c, :, lanes], part_recv.at[step, c, :, lanes], dev(tensor=partner)
        )
        copy.start()
        return copy

    def new_state(frame, mod, step, c, k):
        lanes = pl.ds(k * part_cols, part_cols)
        update = own_part[c, :, lanes] + part_recv[step, c, :, lanes].astype(jnp.float32)
        state = frame[c, block(t), lanes].astype(jnp.float32)
        return (state + mod[2:3, lanes] * update).astype(jnp.bfloat16)

    def move(frame, c, owner, lanes, to):
        region = frame.at[c, block(owner), lanes]
        copy = remote(region, region, to)
        copy.start()
        return copy

    partner = jnp.bitwise_xor(t, 1)
    WAYS = (1, -1)

    class Gather:
        def __init__(self, frame, c, k, side, cut):
            self.frame, self.c, self.side = frame, c, side
            self.start = k * part_cols
            self.cut = cut

        def cols(self, low, high):
            return pl.ds(self.start + low, high - low)

        def ring(self, owner_x, side, d, low, high):
            owner = tensor_of(owner_x, side)
            return move(self.frame, self.c, owner, self.cols(low, high), dev(tensor=tensor_of(x + d, y)))

        def cross(self, owner_x, low):
            owner = tensor_of(owner_x, self.side)
            return move(self.frame, self.c, owner, self.cols(low, part_cols), dev(tensor=partner))

        def first(self):
            self.across = self.cross(x, 0)
            self.own = [self.ring(x, self.side, d, 0, part_cols) for d in WAYS]

        def second(self):
            self.across.wait_recv()
            self.other = [self.ring(x, 1 - self.side, d, 0, self.cut) for d in WAYS]

        def forward_own(self):
            mid = part_cols // 2
            self.far, self.crossed = [], []
            for copy, d in zip(self.own, WAYS):
                copy.wait_recv()
                low, high = (0, mid) if d == 1 else (mid, part_cols)
                self.far.append(self.ring(x - d, self.side, d, low, high))
                if self.cut < part_cols:
                    self.crossed.append(self.cross(x - d, self.cut))

        def forward_other(self):
            mid = self.cut // 2
            self.far_other = []
            for copy, d in zip(self.other, WAYS):
                copy.wait_recv()
                low, high = (0, mid) if d == 1 else (mid, self.cut)
                self.far_other.append(self.ring(x - d, 1 - self.side, d, low, high))
            if self.cut < part_cols:
                self.far[1].wait_recv()
                self.crossed.append(self.cross(x + 2, self.cut))

        def wait(self):
            self.far[0].wait_recv()
            if self.cut == part_cols:
                self.far[1].wait_recv()
            for copy in self.far_other + self.crossed:
                copy.wait_recv()

    def output_projection(step, exchanged):
        partials = []
        for c in range(chunks):
            for copy in exchanged[c]:
                copy.wait_recv()
            for k in range(parts):
                partials.append(project_out(step, c, k))
        return partials

    def attention(step, position_zero, kv_copies, between=()):
        for c in range(chunks):
            attend_own(c)
            if between and c == 0:
                between[0]()
        for copy in kv_copies:
            copy.wait_recv()
        exchanged = []
        for c in range(chunks):

            @pl.when(position_zero)
            def _():
                attend_alone(step, c)

            @pl.when(jnp.logical_not(position_zero))
            def _():
                attend_prev(step, c)

            exchanged.append(exchange_att(step, c))
            if between and c == 0:
                between[1]()
        return exchanged

    def wait_frame(c):
        @pl.when(q != last)
        def _():
            pltpu.make_async_copy(frame0.at[c], frame0.at[c], load_sem.at[c]).wait()

        @pl.when(q == last)
        def _():
            own_noise[c].wait()
            for cc, k, copy in noise_copies:
                if cc == c:
                    copy.wait_recv()

    wait_frame(0)
    send_mod.wait_recv()
    norm_chunk(frame0, mod_next, 0)
    wo_start()
    for copy in load_kv:
        copy.wait()
    kv_copies = []
    project_kv(0)
    kv_copies.append(send_kv(0, 0))
    for c in range(1, chunks):
        wait_frame(c)
        norm_chunk(frame0, mod_next, c)
        project_kv(c)
        kv_copies.append(send_kv(0, c))
    load_q.wait()
    project_q(0)
    wo_forward()
    for c in range(1, chunks):
        project_q(c)
    exchanged = attention(0, q == last, kv_copies, (wo_forward_far, wo_other_side))
    wo_finish()
    partials = output_projection(0, exchanged)

    def send_shifted(u):
        c, k = units[u]
        lanes = pl.ds(k * part_cols, part_cols)
        partials[u].wait_recv()
        z_send[c, :, lanes] = new_state(frame0, mod_next, 0, c, k)
        place = frame1.at[c, block(t), lanes]
        to = dev(queue_at(2), partner)
        copy = remote(z_send.at[c, :, lanes], place, to)
        counter[0] -= 1
        entering = remote(noise.at[1, pl.ds(c * rows, rows), lanes], place, to, keep=False)

        @pl.when(q == last - 1)
        def _():
            entering.start()

        @pl.when(q != last - 1)
        def _():
            copy.start()

        return copy

    n_units = len(units)
    shifted = [None] * n_units
    gathers = [Gather(frame1, c, k, 1 - y, part_cols) for c, k in units]

    def first_after_shift(u):
        shifted[u].wait_recv()
        gathers[u].first()

    for tick in range(n_units + 3):
        if tick < n_units:
            shifted[tick] = send_shifted(tick)
        if 0 <= tick - 1 < n_units:
            first_after_shift(tick - 1)
        if 0 <= tick - 2 < n_units:
            gathers[tick - 2].second()
            gathers[tick - 2].forward_own()
        if 0 <= tick - 3 < n_units - parts:
            gathers[tick - 3].forward_other()

    for copy in kv_copies:
        copy.wait_send()
    sent[:] = [copy for copy in sent if all(copy is not done for done in kv_copies)]
    kv_copies = []
    for c in range(chunks):
        for k in range(parts):
            gathers[c * parts + k].wait()
        norm_chunk(frame1, mod_own, c)
        project_kv(c)
        kv_copies.append(send_kv(1, c))
        if c == chunks - 2:
            for u in range(n_units - parts, n_units):
                gathers[u].forward_other()
        project_q(c)
    exchanged = attention(1, q == 0, kv_copies)
    partials = output_projection(1, exchanged)
    cut = LAST_CUT if part_cols == LAST_PART else part_cols // 2
    gathers = [Gather(frame2, c, k, y, cut) for c, k in units]
    stores = []

    def store(c):
        for k in range(parts):
            gathers[c * parts + k].wait()
        copy = load(frame2.at[c], out.at[c], c)
        copy.start()
        stores.append(copy)

    for tick in range(n_units + 2):
        if tick < n_units:
            c, k = units[tick]
            partials[tick].wait_recv()
            frame2[c, block(t), pl.ds(k * part_cols, part_cols)] = new_state(
                frame1, mod_own, 1, c, k
            )
            gathers[tick].first()
        if 0 <= tick - 1 < n_units:
            gathers[tick - 1].second()
            gathers[tick - 1].forward_own()
        if 0 <= tick - 2 < n_units:
            gathers[tick - 2].forward_other()
    for c in range(chunks):
        store(c)
    for copy in stores:
        copy.wait()
    for copy in sent:
        copy.wait_send()
    for c, k, copy in noise_copies:

        @pl.when(q == noise_from[k, c])
        def _():
            copy.wait_send()


def body(
    latents, levels, mod_table, step_size, qkv_weight, q_gain, k_gain, out_weight, fresh_noise
):
    frame_rows, width = latents.shape[1:]
    cols = qkv_weight.shape[2]
    heads = cols // HD
    n_tensor = lax.axis_size("tensor")
    chunks = CHUNKS
    chunk_rows = frame_rows // chunks
    rows = chunk_rows // n_tensor
    bf16, f32 = jnp.bfloat16, jnp.float32
    frame = pltpu.VMEM((chunks, chunk_rows, width), bf16)
    anywhere = pl.BlockSpec(memory_space=pl.ANY)
    vmem = pl.BlockSpec(memory_space=pltpu.VMEM)
    n_copies = 192
    out = pl.pallas_call(
        kernel,
        out_shape=jax.ShapeDtypeStruct((chunks, chunk_rows, width), bf16),
        in_specs=[pl.BlockSpec(memory_space=pltpu.SMEM)] + [anywhere] * 4 + [vmem] * 4,
        out_specs=anywhere,
        scratch_shapes=[
            frame, frame, frame, frame,
            pltpu.VMEM((width, 2 * cols), bf16),
            pltpu.VMEM((width, cols), bf16),
            pltpu.VMEM((n_tensor // 2 * cols, width), bf16),
            pltpu.VMEM((chunks, chunk_rows, cols), bf16),
            pltpu.VMEM((2, frame_rows, cols), bf16),
            pltpu.VMEM((STEPS, 2, frame_rows, cols), bf16),
            pltpu.VMEM((8, width), f32),
            pltpu.VMEM((8, width), f32),
            pltpu.VMEM((8, HD), f32),
            pltpu.VMEM((chunks, chunk_rows, cols), f32),
            pltpu.VMEM((chunks, heads, chunk_rows, HD), f32),
            pltpu.VMEM((chunks, heads, chunk_rows, HD), f32),
            pltpu.VMEM((STEPS, chunks, chunk_rows, cols), bf16),
            pltpu.VMEM((STEPS, chunks, 2 * rows, n_tensor // 2 * cols), bf16),
            pltpu.VMEM((chunks, rows, width), f32),
            pltpu.VMEM((STEPS, chunks, rows, width), bf16),
            pltpu.VMEM((STEPS, chunks, rows, width), bf16),
            pltpu.VMEM((chunks, rows, width), bf16),
            pltpu.SemaphoreType.DMA((chunks + 4,)),
            pltpu.SemaphoreType.DMA((n_copies,)),
            pltpu.SemaphoreType.DMA((n_copies,)),
        ],
        compiler_params=pltpu.CompilerParams(
            collective_id=0, has_side_effects=True, vmem_limit_bytes=62 * 1024 * 1024
        ),
        name="denoise",
    )(
        levels, latents, fresh_noise, qkv_weight, out_weight, mod_table,
        step_size[None], q_gain[None], k_gain[None],
    )
    out = out.reshape(chunks, n_tensor, rows, width).transpose(1, 0, 2, 3)
    return out.reshape(1, frame_rows, width)


def solution(mesh):
    return jax.shard_map(
        body,
        mesh=mesh,
        in_specs=(
            P("queue", None, None),
            P("queue"),
            P(),
            P(),
            P(None, None, "tensor"),
            P(),
            P(),
            P("tensor", None),
            P(None, "tensor", None),
        ),
        out_specs=P("queue", None, None),
        check_vma=False,
    )
```

```python
import functools
import math

import jax
import jax.numpy as jnp
from jax import lax
from jax.experimental import pallas as pl
from jax.experimental.pallas import tpu as pltpu
from jax.sharding import PartitionSpec as P

HD = 128
STEPS = 2
CHUNKS = 2
PARTS = 2
CUT_PART = 1536
CUT = 1280
MESH = pl.DeviceIdType.MESH
NOISE_FROM = {1: (15, 15), 2: (15, 15), 3: (3, 3), 4: (11, 11), 5: (2, 10), 6: (15, 15), 7: (13, 13)}


def dot(a, b):
    return jnp.dot(a, b, preferred_element_type=jnp.float32)


def kernel(
    levels, lat, noise, wqkv, wout, mod_table, step_size, q_gain, k_gain, frame2,
    frame0, frame1, normed, wkv, wq, wo, q_buf, kv, kv_prev, mod_own, mod_next, gains,
    acc, lowest, top, total, att, att_all, own_part, part_send, part_recv, z_send,
    load_sem, send_sem, recv_sem,
):
    n_queue, n_tensor = lax.axis_size("queue"), lax.axis_size("tensor")
    n_x = n_tensor // 2
    q, t = lax.axis_index("queue"), lax.axis_index("tensor")
    x, y = t // 2, t % 2
    core = q % 2
    chunks, chunk_rows, width = frame0.shape
    rows = chunk_rows // n_tensor
    cols = wq.shape[1]
    heads = cols // HD
    half = width // 2
    last = n_queue - 1
    noise_from = {
        (k, c): (v[c % 2] if v[c % 2] <= last else last)
        for k, v in NOISE_FROM.items()
        for c in range(chunks)
    }

    def dev(queue=None, tensor=None):
        return {"queue": q if queue is None else queue, "tensor": t if tensor is None else tensor}

    def tensor_of(xx, yy):
        return lax.rem(xx + n_x, n_x) * 2 + yy

    def queue_at(d):
        return lax.rem(q + d + n_queue, n_queue)

    counter = [0]
    sent = []

    def remote(src, dst, to, keep=True):
        i = counter[0]
        counter[0] += 1
        copy = pltpu.make_async_remote_copy(
            src_ref=src, dst_ref=dst, send_sem=send_sem.at[i], recv_sem=recv_sem.at[i],
            device_id=to, device_id_type=MESH,
        )
        if keep:
            sent.append(copy)
        return copy

    def block(owner):
        return pl.ds(pl.multiple_of(owner * rows, 16), rows)

    barrier = pltpu.get_barrier_semaphore()
    partners = [dev(tensor=jnp.bitwise_xor(t, k)) for k in range(1, n_tensor)]
    near = {1, n_queue - 1} | ({4, n_queue - 4} if n_queue > 4 else set())
    partners += [dev(queue=queue_at(d)) for d in sorted(near)]
    partners += [dev(queue_at(d), jnp.bitwise_xor(t, 1)) for d in sorted({2, n_queue - 2})]
    for to in partners:
        pl.semaphore_signal(barrier, inc=1, device_id=to, device_id_type=MESH)
    extra = sorted({(k, v) for (k, _), v in noise_from.items() if v != last})
    for k, v in extra:

        @pl.when(q == v)
        def _():
            pl.semaphore_signal(
                barrier, inc=1, device_id=dev(last, jnp.bitwise_xor(t, k)), device_id_type=MESH
            )

        @pl.when(q == last)
        def _():
            pl.semaphore_signal(
                barrier, inc=1, device_id=dev(v, jnp.bitwise_xor(t, k)), device_id_type=MESH
            )

    def load(src, dst, i):
        return pltpu.make_async_copy(src, dst, load_sem.at[i])

    def lat_rows(ref, owner, c):
        return ref.at[0, pl.ds(owner * rows * chunks + c * rows, rows), :]

    own_noise = [
        load(noise.at[0, pl.ds(c * rows, rows), :], frame0.at[c, block(t), :], c)
        for c in range(chunks)
    ]

    @pl.when(q != last)
    def _():
        for owner in range(n_tensor):
            load(lat_rows(lat, owner, 0), frame0.at[0, pl.ds(owner * rows, rows), :], 0).start()

    @pl.when(q == last)
    def _():
        for c in range(chunks):
            own_noise[c].start()

    load_kv = [load(wqkv.at[j + 1], wkv.at[:, pl.ds(j * cols, cols)], chunks + j) for j in range(2)]
    load_q = load(wqkv.at[0], wq, chunks + 2)
    own_wo = pl.ds(pl.multiple_of(x * cols, HD), cols)
    load_o = load(wout, wo.at[own_wo, :], chunks + 3)
    for copy in load_kv:
        copy.start()

    @pl.when(q != last)
    def _():
        for c in range(1, chunks):
            for owner in range(n_tensor):
                load(lat_rows(lat, owner, c), frame0.at[c, pl.ds(owner * rows, rows), :], c).start()

    load_q.start()
    load_o.start()

    n_levels = mod_table.shape[0]
    hot = lax.broadcasted_iota(jnp.int32, (8, n_levels), 1) == levels[0]
    rate = jnp.sum(jnp.where(hot, step_size[...], 0.0), axis=1, keepdims=True)[0:1]
    hot = hot.astype(jnp.float32).astype(jnp.bfloat16)
    mod_own[...] = jnp.zeros_like(mod_own)
    lowest[...] = jnp.full(lowest.shape, -3e38, jnp.float32)
    mod_own[0:1, :] = dot(hot, mod_table[:, :width])[0:1]
    mod_own[1:2, :] = 1.0 + dot(hot, mod_table[:, width : 2 * width])[0:1]
    mod_own[2:3, :] = rate * dot(hot, mod_table[:, 2 * width :])[0:1]
    gains[0:1, :] = q_gain[...] * (math.log2(math.e) / math.sqrt(HD))
    gains[1:2, :] = k_gain[...]

    arrivals = len(partners)
    for _, v in extra:
        arrivals = arrivals + (q == v).astype(jnp.int32) + (q == last).astype(jnp.int32)
    pl.semaphore_wait(barrier, arrivals)

    send_mod = remote(mod_own, mod_next, dev(queue=queue_at(-1)))
    send_mod.start()
    noise_copies = []
    for c in range(chunks):
        for k in range(1, n_tensor):
            copy = remote(
                noise.at[0, pl.ds(c * rows, rows), :], frame0.at[c, block(t), :],
                dev(last, jnp.bitwise_xor(t, k)), keep=False,
            )
            noise_copies.append((c, k, copy))

            @pl.when(q == noise_from[k, c])
            def _():
                copy.start()

    n_z = n_queue // 4
    z_side = (q // 4) % 2 if n_z > 1 else 0
    sides = 2 if n_z > 1 else 1
    share = width // (2 * sides)

    def share_cols(side, part=None):
        start = (side * 2 + core) * share
        if part is None:
            return pl.ds(pl.multiple_of(start, HD), share)
        return pl.ds(pl.multiple_of(start + part * (share // 2), HD), share // 2)

    def wo_region(xx, side, part=None, row_part=None):
        start, size = lax.rem(xx + n_x, n_x) * cols, cols
        if row_part is not None:
            start, size = start + row_part * (cols // 2), cols // 2
        return wo.at[pl.ds(pl.multiple_of(start, 16), size), share_cols(side, part)]

    other_core = q + 1 - 2 * core
    z_ways = (4, -4)
    wo_direct, wo_far, wo_pass, wo_z = [], [], [], []

    def wo_move(region, to, into):
        copy = remote(region, region, to)
        copy.start()
        into.append(copy)

    def wo_start():
        for d in (1, -1):
            copy = remote(
                wout.at[:, share_cols(z_side)], wo.at[own_wo, share_cols(z_side)],
                dev(tensor=tensor_of(x + d, y)),
            )
            copy.start()
            wo_direct.append(copy)

    def wo_forward():
        for i, d in enumerate((1, -1)):
            wo_direct[i].wait_recv()
            wo_move(wo_region(x - d, z_side, part=i), dev(tensor=tensor_of(x + d, y)), wo_far)
            if sides == 2:
                for e, dz in enumerate(z_ways):
                    wo_move(wo_region(x - d, z_side, row_part=e), dev(queue=queue_at(dz)), wo_z)
            wo_move(wo_region(x - d, z_side), dev(queue=other_core), wo_pass)

    def wo_forward_far():
        for i in range(2):
            wo_far[i].wait_recv()
            if sides == 2:
                wo_move(wo_region(x + 2, z_side, part=i), dev(queue=queue_at(z_ways[i])), wo_z)
        wo_move(wo_region(x + 2, z_side), dev(queue=other_core), wo_pass)

    def wo_other_side():
        if sides == 2:
            for i, xx in enumerate((x - 1, x + 1, x + 2)):
                for e in range(2):
                    wo_z[2 * i + e].wait_recv()
                wo_move(wo_region(xx, 1 - z_side), dev(queue=other_core), wo_pass)

    def wo_finish():
        for copy in wo_pass:
            copy.wait_recv()
        load_o.wait()

    def norm_chunk(frame, mod, c):
        tile = chunk_rows // 2

        def step(i, _):
            at = pl.ds(pl.multiple_of(i * tile, 16), tile)
            state = frame[c, at, :].astype(jnp.float32)
            scale = lax.rsqrt(jnp.mean(state * state, axis=-1, keepdims=True) + 1e-06)
            normed[c, at, :] = (state * scale * mod[1:2, :] + mod[0:1, :]).astype(jnp.bfloat16)
            return 0

        lax.fori_loop(0, chunk_rows // tile, step, 0)

    def head_norm(part, gain):
        scale = lax.rsqrt(jnp.mean(part * part, axis=-1, keepdims=True) + 1e-06)
        return (part * scale * gain).astype(jnp.bfloat16)

    def project_kv(c):
        at = pl.ds(c * chunk_rows, chunk_rows)
        both = dot(normed[c], wkv[...])
        for h in range(heads):
            lanes = slice(h * HD, (h + 1) * HD)
            kv[0, at, lanes] = head_norm(both[:, lanes], gains[1:2, :])
        kv[1, at, :] = both[:, cols:].astype(jnp.bfloat16)

    def project_q(c):
        part = dot(normed[c], wq[...])
        for h in range(heads):
            lanes = slice(h * HD, (h + 1) * HD)
            q_buf[c, :, lanes] = head_norm(part[:, lanes], gains[0:1, :])

    def send_kv(step, c):
        at = pl.ds(c * chunk_rows, chunk_rows)
        copy = remote(kv.at[:, at, :], kv_prev.at[step, :, at, :], dev(queue=queue_at(1)))
        copy.start()
        return copy

    def attend(c, h, keys, values, before):
        lanes = slice(h * HD, (h + 1) * HD)
        logits = lax.dot_general(
            q_buf[c, :, lanes], keys[:, lanes], (((1,), (1,)), ((), ())),
            preferred_element_type=jnp.float32,
        )
        peak = jnp.max(logits, axis=-1, keepdims=True)
        peak = jnp.maximum(before, jnp.broadcast_to(peak, (chunk_rows, HD)))
        tiled = jnp.concatenate([peak] * (logits.shape[1] // HD), axis=1)
        raised = jnp.exp2(logits - tiled).astype(jnp.bfloat16)
        ones = jnp.ones((values.shape[0], HD), jnp.bfloat16)
        both = dot(raised, jnp.concatenate([values[:, lanes], ones], axis=1))
        return both[:, :HD], both[:, HD:], peak

    def attend_own(c):
        for h in range(heads):
            summed, weight, peak = attend(c, h, kv.at[0], kv.at[1], lowest[...])
            acc[c, :, h * HD : (h + 1) * HD] = summed
            total[c, h] = weight
            top[c, h] = peak

    def attend_prev(step, c):
        for h in range(heads):
            lanes = slice(h * HD, (h + 1) * HD)
            before = top[c, h]
            summed, weight, peak = attend(
                c, h, kv_prev.at[step, 0], kv_prev.at[step, 1], before
            )
            fade = jnp.exp2(before - peak)
            weight = total[c, h] * fade + weight
            summed = acc[c, :, lanes] * fade + summed
            att[step, c, :, lanes] = (summed / weight).astype(jnp.bfloat16)

    def attend_alone(step, c):
        for h in range(heads):
            lanes = slice(h * HD, (h + 1) * HD)
            att[step, c, :, lanes] = (acc[c, :, lanes] / total[c, h]).astype(jnp.bfloat16)

    def exchange_att(step, c):
        mine = pl.ds(pl.multiple_of(x * cols, HD), cols)
        copies = []
        for d in range(1, n_x):
            xx = lax.rem(x + d, n_x)
            at = pl.ds(pl.multiple_of(xx * 2 * rows, 16), 2 * rows)
            copy = remote(
                att.at[step, c, at, :], att_all.at[step, c, :, mine],
                dev(tensor=tensor_of(xx, y)),
            )
            copy.start()
            copies.append(copy)
        at = pl.ds(pl.multiple_of(x * 2 * rows, 16), 2 * rows)
        att_all[step, c, :, mine] = att[step, c, at, :]
        return copies

    parts = PARTS
    part_cols = width // parts
    units = [(c, k) for c in range(chunks) for k in range(parts)]

    def project_out(step, c, k):
        lanes = pl.ds(k * part_cols, part_cols)
        part = dot(att_all[step, c], wo[:, lanes])
        low, high = part[:rows], part[rows:]
        own_part[c, :, lanes] = jnp.where(y == 0, low, high)
        part_send[step, c, :, lanes] = jnp.where(y == 0, high, low).astype(jnp.bfloat16)
        copy = remote(
            part_send.at[step, c, :, lanes], part_recv.at[step, c, :, lanes], dev(tensor=partner)
        )
        copy.start()
        return copy

    def new_state(frame, mod, step, c, k):
        lanes = pl.ds(k * part_cols, part_cols)
        update = own_part[c, :, lanes] + part_recv[step, c, :, lanes].astype(jnp.float32)
        state = frame[c, block(t), lanes].astype(jnp.float32)
        return (state + mod[2:3, lanes] * update).astype(jnp.bfloat16)

    def move(frame, c, owner, lanes, to):
        region = frame.at[c, block(owner), lanes]
        copy = remote(region, region, to)
        copy.start()
        return copy

    partner = jnp.bitwise_xor(t, 1)
    WAYS = (1, -1)

    class Gather:
        def __init__(self, frame, c, k, side, cut):
            self.frame, self.c, self.side = frame, c, side
            self.start = k * part_cols
            self.cut = cut

        def cols(self, low, high):
            return pl.ds(self.start + low, high - low)

        def ring(self, owner_x, side, d, low, high):
            owner = tensor_of(owner_x, side)
            return move(self.frame, self.c, owner, self.cols(low, high), dev(tensor=tensor_of(x + d, y)))

        def cross(self, owner_x, low):
            owner = tensor_of(owner_x, self.side)
            return move(self.frame, self.c, owner, self.cols(low, part_cols), dev(tensor=partner))

        def first(self):
            self.across = self.cross(x, 0)
            self.own = [self.ring(x, self.side, d, 0, part_cols) for d in WAYS]

        def second(self):
            self.across.wait_recv()
            self.other = [self.ring(x, 1 - self.side, d, 0, self.cut) for d in WAYS]

        def forward_own(self):
            mid = part_cols // 2
            self.far, self.crossed = [], []
            for copy, d in zip(self.own, WAYS):
                copy.wait_recv()
                low, high = (0, mid) if d == 1 else (mid, part_cols)
                self.far.append(self.ring(x - d, self.side, d, low, high))
                if self.cut < part_cols:
                    self.crossed.append(self.cross(x - d, self.cut))

        def forward_other(self):
            mid = self.cut // 2
            self.far_other = []
            for copy, d in zip(self.other, WAYS):
                copy.wait_recv()
                low, high = (0, mid) if d == 1 else (mid, self.cut)
                self.far_other.append(self.ring(x - d, 1 - self.side, d, low, high))
            if self.cut < part_cols:
                self.far[1].wait_recv()
                self.crossed.append(self.cross(x + 2, self.cut))

        def wait(self):
            self.far[0].wait_recv()
            if self.cut == part_cols:
                self.far[1].wait_recv()
            for copy in self.far_other + self.crossed:
                copy.wait_recv()

    def output_projection(step, exchanged):
        partials = []
        for c in range(chunks):
            for copy in exchanged[c]:
                copy.wait_recv()
            for k in range(parts):
                partials.append(project_out(step, c, k))
        return partials

    def attention(step, position_zero, kv_copies, between=()):
        for c in range(chunks):
            attend_own(c)
            if between and c == 0:
                between[0]()
        for copy in kv_copies:
            copy.wait_recv()
        exchanged = []
        for c in range(chunks):

            @pl.when(position_zero)
            def _():
                attend_alone(step, c)

            @pl.when(jnp.logical_not(position_zero))
            def _():
                attend_prev(step, c)

            exchanged.append(exchange_att(step, c))
            if between and c == 0:
                between[1]()
        return exchanged

    def wait_frame(c):
        @pl.when(q != last)
        def _():
            pltpu.make_async_copy(frame0.at[c], frame0.at[c], load_sem.at[c]).wait()

        @pl.when(q == last)
        def _():
            own_noise[c].wait()
            for cc, k, copy in noise_copies:
                if cc == c:
                    copy.wait_recv()

    wait_frame(0)
    send_mod.wait_recv()
    norm_chunk(frame0, mod_next, 0)
    wo_start()
    for copy in load_kv:
        copy.wait()
    kv_copies = []
    project_kv(0)
    kv_copies.append(send_kv(0, 0))
    for c in range(1, chunks):
        wait_frame(c)
        norm_chunk(frame0, mod_next, c)
        project_kv(c)
        kv_copies.append(send_kv(0, c))
    load_q.wait()
    project_q(0)
    wo_forward()
    for c in range(1, chunks):
        project_q(c)
    exchanged = attention(0, q == last, kv_copies, (wo_forward_far, wo_other_side))
    wo_finish()
    partials = output_projection(0, exchanged)

    def send_shifted(u):
        c, k = units[u]
        lanes = pl.ds(k * part_cols, part_cols)
        partials[u].wait_recv()
        z_send[c, :, lanes] = new_state(frame0, mod_next, 0, c, k)
        place = frame1.at[c, block(t), lanes]
        to = dev(queue_at(2), partner)
        copy = remote(z_send.at[c, :, lanes], place, to)
        counter[0] -= 1
        entering = remote(noise.at[1, pl.ds(c * rows, rows), lanes], place, to, keep=False)

        @pl.when(q == last - 1)
        def _():
            entering.start()

        @pl.when(q != last - 1)
        def _():
            copy.start()

        return copy

    n_units = len(units)
    shifted = [None] * n_units
    cut = CUT if part_cols == CUT_PART else part_cols // 2
    gathers = [Gather(frame1, c, k, 1 - y, part_cols) for c, k in units]

    def first_after_shift(u):
        shifted[u].wait_recv()
        gathers[u].first()

    for tick in range(n_units + 3):
        if tick < n_units:
            shifted[tick] = send_shifted(tick)
        if 0 <= tick - 1 < n_units:
            first_after_shift(tick - 1)
        if 0 <= tick - 2 < n_units:
            gathers[tick - 2].second()
            gathers[tick - 2].forward_own()
        if 0 <= tick - 3 < parts:
            gathers[tick - 3].forward_other()

    for copy in kv_copies:
        copy.wait_send()
    sent[:] = [copy for copy in sent if all(copy is not done for done in kv_copies)]
    kv_copies = []
    for c in range(chunks):
        if c + 1 < chunks and chunks > 2:
            for k in range(parts):
                gathers[(c + 1) * parts + k].forward_other()
        for k in range(parts):
            gathers[c * parts + k].wait()
        norm_chunk(frame1, mod_own, c)
        project_kv(c)
        kv_copies.append(send_kv(1, c))
        if c + 1 < chunks and chunks == 2:
            for k in range(parts):
                gathers[(c + 1) * parts + k].forward_other()
        project_q(c)
    exchanged = attention(1, q == 0, kv_copies)
    partials = output_projection(1, exchanged)
    gathers = [Gather(frame2, c, k, y, cut) for c, k in units]

    for tick in range(n_units + 2):
        if tick < n_units:
            c, k = units[tick]
            partials[tick].wait_recv()
            frame2[c, block(t), pl.ds(k * part_cols, part_cols)] = new_state(
                frame1, mod_own, 1, c, k
            )
            gathers[tick].first()
        if 0 <= tick - 1 < n_units:
            gathers[tick - 1].second()
            gathers[tick - 1].forward_own()
        if 0 <= tick - 2 < n_units:
            gathers[tick - 2].forward_other()
    for gather in gathers:
        gather.wait()
    for copy in sent:
        copy.wait_send()
    for c, k, copy in noise_copies:

        @pl.when(q == noise_from[k, c])
        def _():
            copy.wait_send()


def body(
    latents, levels, mod_table, step_size, qkv_weight, q_gain, k_gain, out_weight, fresh_noise
):
    frame_rows, width = latents.shape[1:]
    cols = qkv_weight.shape[2]
    heads = cols // HD
    n_tensor = lax.axis_size("tensor")
    chunks = CHUNKS
    chunk_rows = frame_rows // chunks
    rows = chunk_rows // n_tensor
    bf16, f32 = jnp.bfloat16, jnp.float32
    frame = pltpu.VMEM((chunks, chunk_rows, width), bf16)
    anywhere = pl.BlockSpec(memory_space=pl.ANY)
    vmem = pl.BlockSpec(memory_space=pltpu.VMEM)
    n_copies = 256
    out = pl.pallas_call(
        kernel,
        out_shape=pltpu.VMEM((chunks, chunk_rows, width), bf16),
        in_specs=[pl.BlockSpec(memory_space=pltpu.SMEM)] + [anywhere] * 4 + [vmem] * 4,
        out_specs=vmem,
        scratch_shapes=[
            frame, frame, frame,
            pltpu.VMEM((width, 2 * cols), bf16),
            pltpu.VMEM((width, cols), bf16),
            pltpu.VMEM((n_tensor // 2 * cols, width), bf16),
            pltpu.VMEM((chunks, chunk_rows, cols), bf16),
            pltpu.VMEM((2, frame_rows, cols), bf16),
            pltpu.VMEM((STEPS, 2, frame_rows, cols), bf16),
            pltpu.VMEM((8, width), f32),
            pltpu.VMEM((8, width), f32),
            pltpu.VMEM((8, HD), f32),
            pltpu.VMEM((chunks, chunk_rows, cols), f32),
            pltpu.VMEM((chunk_rows, HD), f32),
            pltpu.VMEM((chunks, heads, chunk_rows, HD), f32),
            pltpu.VMEM((chunks, heads, chunk_rows, HD), f32),
            pltpu.VMEM((STEPS, chunks, chunk_rows, cols), bf16),
            pltpu.VMEM((STEPS, chunks, 2 * rows, n_tensor // 2 * cols), bf16),
            pltpu.VMEM((chunks, rows, width), f32),
            pltpu.VMEM((STEPS, chunks, rows, width), bf16),
            pltpu.VMEM((STEPS, chunks, rows, width), bf16),
            pltpu.VMEM((chunks, rows, width), bf16),
            pltpu.SemaphoreType.DMA((chunks + 4,)),
            pltpu.SemaphoreType.DMA((n_copies,)),
            pltpu.SemaphoreType.DMA((n_copies,)),
        ],
        compiler_params=pltpu.CompilerParams(
            collective_id=0, has_side_effects=True, vmem_limit_bytes=54 * 1024 * 1024
        ),
        name="denoise",
    )(
        levels, latents, fresh_noise, qkv_weight, out_weight, mod_table,
        step_size[None], q_gain[None], k_gain[None],
    )
    out = out.reshape(chunks, n_tensor, rows, width).transpose(1, 0, 2, 3)
    return out.reshape(1, frame_rows, width)


def solution(mesh):
    return jax.shard_map(
        body,
        mesh=mesh,
        in_specs=(
            P("queue", None, None),
            P("queue"),
            P(),
            P(),
            P(None, None, "tensor"),
            P(),
            P(),
            P("tensor", None),
            P(None, "tensor", None),
        ),
        out_specs=P("queue", None, None),
        check_vma=False,
    )
```

```python
import functools
import math

import jax
import jax.numpy as jnp
from jax import lax
from jax.experimental import pallas as pl
from jax.experimental.pallas import tpu as pltpu
from jax.sharding import PartitionSpec as P

HD = 128
STEPS = 2
CHUNKS = 2
PARTS = 2
CUT_PART = 1536
CUT = 1280
MESH = pl.DeviceIdType.MESH
NOISE_FROM = {1: (15, 15), 2: (15, 15), 3: (3, 3), 4: (11, 11), 5: (2, 10), 6: (15, 15), 7: (13, 13)}


def dot(a, b):
    return jnp.dot(a, b, preferred_element_type=jnp.float32)


def kernel(
    levels, lat, noise, wqkv, wout, mod_table, step_size, q_gain, k_gain, frame2,
    frame0, frame1, normed, wkv, wq, wo, q_buf, kv, kv_prev, mod_own, mod_next, gains,
    acc, lowest, top, total, att, att_all, own_part, part_send, part_recv, z_send,
    load_sem, send_sem, recv_sem,
):
    n_queue, n_tensor = lax.axis_size("queue"), lax.axis_size("tensor")
    n_x = n_tensor // 2
    q, t = lax.axis_index("queue"), lax.axis_index("tensor")
    x, y = t // 2, t % 2
    core = q % 2
    chunks, chunk_rows, width = frame0.shape
    rows = chunk_rows // n_tensor
    cols = wq.shape[1]
    heads = cols // HD
    half = width // 2
    last = n_queue - 1
    noise_from = {
        (k, c): (v[c % 2] if v[c % 2] <= last else last)
        for k, v in NOISE_FROM.items()
        for c in range(chunks)
    }

    def dev(queue=None, tensor=None):
        return {"queue": q if queue is None else queue, "tensor": t if tensor is None else tensor}

    def tensor_of(xx, yy):
        return lax.rem(xx + n_x, n_x) * 2 + yy

    def queue_at(d):
        return lax.rem(q + d + n_queue, n_queue)

    counter = [0]
    sent = []

    def remote(src, dst, to, keep=True):
        i = counter[0]
        counter[0] += 1
        copy = pltpu.make_async_remote_copy(
            src_ref=src, dst_ref=dst, send_sem=send_sem.at[i], recv_sem=recv_sem.at[i],
            device_id=to, device_id_type=MESH,
        )
        if keep:
            sent.append(copy)
        return copy

    def block(owner):
        return pl.ds(pl.multiple_of(owner * rows, 16), rows)

    barrier = pltpu.get_barrier_semaphore()
    partners = [dev(tensor=jnp.bitwise_xor(t, k)) for k in range(1, n_tensor)]
    near = {1, n_queue - 1} | ({4, n_queue - 4} if n_queue > 4 else set())
    partners += [dev(queue=queue_at(d)) for d in sorted(near)]
    partners += [dev(queue_at(d), jnp.bitwise_xor(t, 1)) for d in sorted({2, n_queue - 2})]
    for to in partners:
        pl.semaphore_signal(barrier, inc=1, device_id=to, device_id_type=MESH)
    extra = sorted({(k, v) for (k, _), v in noise_from.items() if v != last})
    for k, v in extra:

        @pl.when(q == v)
        def _():
            pl.semaphore_signal(
                barrier, inc=1, device_id=dev(last, jnp.bitwise_xor(t, k)), device_id_type=MESH
            )

        @pl.when(q == last)
        def _():
            pl.semaphore_signal(
                barrier, inc=1, device_id=dev(v, jnp.bitwise_xor(t, k)), device_id_type=MESH
            )

    def load(src, dst, i):
        return pltpu.make_async_copy(src, dst, load_sem.at[i])

    def lat_rows(ref, owner, c):
        return ref.at[0, pl.ds(owner * rows * chunks + c * rows, rows), :]

    own_noise = [
        load(noise.at[0, pl.ds(c * rows, rows), :], frame0.at[c, block(t), :], c)
        for c in range(chunks)
    ]

    @pl.when(q != last)
    def _():
        for owner in range(n_tensor):
            load(lat_rows(lat, owner, 0), frame0.at[0, pl.ds(owner * rows, rows), :], 0).start()

    @pl.when(q == last)
    def _():
        for c in range(chunks):
            own_noise[c].start()

    load_kv = [load(wqkv.at[j + 1], wkv.at[:, pl.ds(j * cols, cols)], chunks + j) for j in range(2)]
    load_q = load(wqkv.at[0], wq, chunks + 2)
    own_wo = pl.ds(pl.multiple_of(x * cols, HD), cols)
    load_o = load(wout, wo.at[own_wo, :], chunks + 3)
    for copy in load_kv:
        copy.start()

    @pl.when(q != last)
    def _():
        for c in range(1, chunks):
            for owner in range(n_tensor):
                load(lat_rows(lat, owner, c), frame0.at[c, pl.ds(owner * rows, rows), :], c).start()

    load_q.start()
    load_o.start()

    n_levels = mod_table.shape[0]
    hot = lax.broadcasted_iota(jnp.int32, (8, n_levels), 1) == levels[0]
    rate = jnp.sum(jnp.where(hot, step_size[...], 0.0), axis=1, keepdims=True)[0:1]
    hot = hot.astype(jnp.float32).astype(jnp.bfloat16)
    mod_own[...] = jnp.zeros_like(mod_own)
    lowest[...] = jnp.full(lowest.shape, -3e38, jnp.float32)
    mod_own[0:1, :] = dot(hot, mod_table[:, :width])[0:1]
    mod_own[1:2, :] = 1.0 + dot(hot, mod_table[:, width : 2 * width])[0:1]
    mod_own[2:3, :] = rate * dot(hot, mod_table[:, 2 * width :])[0:1]
    gains[0:1, :] = q_gain[...] * (math.log2(math.e) / math.sqrt(HD))
    gains[1:2, :] = k_gain[...]

    arrivals = len(partners)
    for _, v in extra:
        arrivals = arrivals + (q == v).astype(jnp.int32) + (q == last).astype(jnp.int32)
    pl.semaphore_wait(barrier, arrivals)

    send_mod = remote(mod_own, mod_next, dev(queue=queue_at(-1)))
    send_mod.start()
    noise_copies = []
    for c in range(chunks):
        for k in range(1, n_tensor):
            copy = remote(
                noise.at[0, pl.ds(c * rows, rows), :], frame0.at[c, block(t), :],
                dev(last, jnp.bitwise_xor(t, k)), keep=False,
            )
            noise_copies.append((c, k, copy))

            @pl.when(q == noise_from[k, c])
            def _():
                copy.start()

    n_z = n_queue // 4
    z_side = (q // 4) % 2 if n_z > 1 else 0
    sides = 2 if n_z > 1 else 1
    share = width // (2 * sides)

    def share_cols(side, part=None):
        start = (side * 2 + core) * share
        if part is None:
            return pl.ds(pl.multiple_of(start, HD), share)
        return pl.ds(pl.multiple_of(start + part * (share // 2), HD), share // 2)

    def wo_region(xx, side, part=None, row_part=None):
        start, size = lax.rem(xx + n_x, n_x) * cols, cols
        if row_part is not None:
            start, size = start + row_part * (cols // 2), cols // 2
        return wo.at[pl.ds(pl.multiple_of(start, 16), size), share_cols(side, part)]

    other_core = q + 1 - 2 * core
    z_ways = (4, -4)
    wo_direct, wo_far, wo_pass, wo_z = [], [], [], []

    def wo_move(region, to, into):
        copy = remote(region, region, to)
        copy.start()
        into.append(copy)

    def wo_start():
        for e in range(2):
            row_half = pl.ds(e * (cols // 2), cols // 2)
            for d in (1, -1):
                copy = remote(
                    wout.at[row_half, share_cols(z_side)], wo_region(x, z_side, row_part=e),
                    dev(tensor=tensor_of(x + d, y)),
                )
                copy.start()
                wo_direct.append(copy)

    def wo_forward(e):
        for i, d in enumerate((1, -1)):
            wo_direct[2 * e + i].wait_recv()
            wo_move(
                wo_region(x - d, z_side, part=i, row_part=e), dev(tensor=tensor_of(x + d, y)), wo_far
            )
            region = wo_region(x - d, z_side, row_part=e)
            if sides == 2:
                wo_move(region, dev(queue=queue_at(z_ways[(i + e) % 2])), wo_z)
            wo_move(region, dev(queue=other_core), wo_pass)

    def wo_forward_far():
        for i in range(2):
            for e in range(2):
                wo_far[2 * e + i].wait_recv()
            if sides == 2:
                wo_move(wo_region(x + 2, z_side, part=i), dev(queue=queue_at(z_ways[i])), wo_z)
        wo_move(wo_region(x + 2, z_side), dev(queue=other_core), wo_pass)

    def wo_other_side():
        for copy in wo_z:
            copy.wait_recv()
        if sides == 2:
            for xx in (x - 1, x + 1, x + 2):
                wo_move(wo_region(xx, 1 - z_side), dev(queue=other_core), wo_pass)

    def wo_finish():
        for copy in wo_pass:
            copy.wait_recv()
        load_o.wait()

    def norm_chunk(frame, mod, c):
        tile = chunk_rows // 2

        def step(i, _):
            at = pl.ds(pl.multiple_of(i * tile, 16), tile)
            state = frame[c, at, :].astype(jnp.float32)
            scale = lax.rsqrt(jnp.mean(state * state, axis=-1, keepdims=True) + 1e-06)
            normed[c, at, :] = (state * scale * mod[1:2, :] + mod[0:1, :]).astype(jnp.bfloat16)
            return 0

        lax.fori_loop(0, chunk_rows // tile, step, 0)

    def head_norm(part, gain):
        scale = lax.rsqrt(jnp.mean(part * part, axis=-1, keepdims=True) + 1e-06)
        return (part * scale * gain).astype(jnp.bfloat16)

    def project_kv(c):
        at = pl.ds(c * chunk_rows, chunk_rows)
        both = dot(normed[c], wkv[...])
        for h in range(heads):
            lanes = slice(h * HD, (h + 1) * HD)
            kv[0, at, lanes] = head_norm(both[:, lanes], gains[1:2, :])
        kv[1, at, :] = both[:, cols:].astype(jnp.bfloat16)

    def project_q(c):
        part = dot(normed[c], wq[...])
        for h in range(heads):
            lanes = slice(h * HD, (h + 1) * HD)
            q_buf[c, :, lanes] = head_norm(part[:, lanes], gains[0:1, :])

    def send_kv(step, c):
        at = pl.ds(c * chunk_rows, chunk_rows)
        copy = remote(kv.at[:, at, :], kv_prev.at[step, :, at, :], dev(queue=queue_at(1)))
        copy.start()
        return copy

    def attend(c, h, keys, values, before):
        lanes = slice(h * HD, (h + 1) * HD)
        logits = lax.dot_general(
            q_buf[c, :, lanes], keys[:, lanes], (((1,), (1,)), ((), ())),
            preferred_element_type=jnp.float32,
        )
        peak = jnp.max(logits, axis=-1, keepdims=True)
        peak = jnp.maximum(before, jnp.broadcast_to(peak, (chunk_rows, HD)))
        tiled = jnp.concatenate([peak] * (logits.shape[1] // HD), axis=1)
        raised = jnp.exp2(logits - tiled).astype(jnp.bfloat16)
        ones = jnp.ones((values.shape[0], HD), jnp.bfloat16)
        both = dot(raised, jnp.concatenate([values[:, lanes], ones], axis=1))
        return both[:, :HD], both[:, HD:], peak

    def attend_own(c):
        for h in range(heads):
            summed, weight, peak = attend(c, h, kv.at[0], kv.at[1], lowest[...])
            acc[c, :, h * HD : (h + 1) * HD] = summed
            total[c, h] = weight
            top[c, h] = peak

    def attend_prev(step, c):
        for h in range(heads):
            lanes = slice(h * HD, (h + 1) * HD)
            before = top[c, h]
            summed, weight, peak = attend(
                c, h, kv_prev.at[step, 0], kv_prev.at[step, 1], before
            )
            fade = jnp.exp2(before - peak)
            weight = total[c, h] * fade + weight
            summed = acc[c, :, lanes] * fade + summed
            att[step, c, :, lanes] = (summed / weight).astype(jnp.bfloat16)

    def attend_alone(step, c):
        for h in range(heads):
            lanes = slice(h * HD, (h + 1) * HD)
            att[step, c, :, lanes] = (acc[c, :, lanes] / total[c, h]).astype(jnp.bfloat16)

    def exchange_att(step, c):
        mine = pl.ds(pl.multiple_of(x * cols, HD), cols)
        copies = []
        for d in range(1, n_x):
            xx = lax.rem(x + d, n_x)
            at = pl.ds(pl.multiple_of(xx * 2 * rows, 16), 2 * rows)
            copy = remote(
                att.at[step, c, at, :], att_all.at[step, c, :, mine],
                dev(tensor=tensor_of(xx, y)),
            )
            copy.start()
            copies.append(copy)
        at = pl.ds(pl.multiple_of(x * 2 * rows, 16), 2 * rows)
        att_all[step, c, :, mine] = att[step, c, at, :]
        return copies

    parts = PARTS
    part_cols = width // parts
    units = [(c, k) for c in range(chunks) for k in range(parts)]

    def project_out(step, c, k):
        lanes = pl.ds(k * part_cols, part_cols)
        part = dot(att_all[step, c], wo[:, lanes])
        low, high = part[:rows], part[rows:]
        own_part[c, :, lanes] = jnp.where(y == 0, low, high)
        part_send[step, c, :, lanes] = jnp.where(y == 0, high, low).astype(jnp.bfloat16)
        copy = remote(
            part_send.at[step, c, :, lanes], part_recv.at[step, c, :, lanes], dev(tensor=partner)
        )
        copy.start()
        return copy

    def new_state(frame, mod, step, c, k):
        lanes = pl.ds(k * part_cols, part_cols)
        update = own_part[c, :, lanes] + part_recv[step, c, :, lanes].astype(jnp.float32)
        state = frame[c, block(t), lanes].astype(jnp.float32)
        return (state + mod[2:3, lanes] * update).astype(jnp.bfloat16)

    def move(frame, c, owner, lanes, to):
        region = frame.at[c, block(owner), lanes]
        copy = remote(region, region, to)
        copy.start()
        return copy

    partner = jnp.bitwise_xor(t, 1)
    WAYS = (1, -1)

    class Gather:
        def __init__(self, frame, c, k, side, cut):
            self.frame, self.c, self.side = frame, c, side
            self.start = k * part_cols
            self.cut = cut

        def cols(self, low, high):
            return pl.ds(self.start + low, high - low)

        def ring(self, owner_x, side, d, low, high):
            owner = tensor_of(owner_x, side)
            return move(self.frame, self.c, owner, self.cols(low, high), dev(tensor=tensor_of(x + d, y)))

        def cross(self, owner_x, low):
            owner = tensor_of(owner_x, self.side)
            return move(self.frame, self.c, owner, self.cols(low, part_cols), dev(tensor=partner))

        def first(self):
            self.across = self.cross(x, 0)
            self.own = [self.ring(x, self.side, d, 0, part_cols) for d in WAYS]

        def second(self):
            self.across.wait_recv()
            self.other = [self.ring(x, 1 - self.side, d, 0, self.cut) for d in WAYS]

        def forward_own(self):
            mid = part_cols // 2
            self.far, self.crossed = [], []
            for copy, d in zip(self.own, WAYS):
                copy.wait_recv()
                low, high = (0, mid) if d == 1 else (mid, part_cols)
                self.far.append(self.ring(x - d, self.side, d, low, high))
                if self.cut < part_cols:
                    self.crossed.append(self.cross(x - d, self.cut))

        def forward_other(self):
            mid = self.cut // 2
            self.far_other = []
            for copy, d in zip(self.other, WAYS):
                copy.wait_recv()
                low, high = (0, mid) if d == 1 else (mid, self.cut)
                self.far_other.append(self.ring(x - d, 1 - self.side, d, low, high))
            if self.cut < part_cols:
                self.far[1].wait_recv()
                self.crossed.append(self.cross(x + 2, self.cut))

        def wait(self):
            self.far[0].wait_recv()
            if self.cut == part_cols:
                self.far[1].wait_recv()
            for copy in self.far_other + self.crossed:
                copy.wait_recv()

    def output_projection(step, exchanged):
        partials = []
        for c in range(chunks):
            for copy in exchanged[c]:
                copy.wait_recv()
            for k in range(parts):
                partials.append(project_out(step, c, k))
        return partials

    def attention(step, position_zero, kv_copies, between=None):
        for c in range(chunks):
            attend_own(c)
            if between is not None and c == 0:
                between()
        for copy in kv_copies:
            copy.wait_recv()
        exchanged = []
        for c in range(chunks):

            @pl.when(position_zero)
            def _():
                attend_alone(step, c)

            @pl.when(jnp.logical_not(position_zero))
            def _():
                attend_prev(step, c)

            exchanged.append(exchange_att(step, c))
        return exchanged

    def wait_frame(c):
        @pl.when(q != last)
        def _():
            pltpu.make_async_copy(frame0.at[c], frame0.at[c], load_sem.at[c]).wait()

        @pl.when(q == last)
        def _():
            own_noise[c].wait()
            for cc, k, copy in noise_copies:
                if cc == c:
                    copy.wait_recv()

    wo_start()
    wait_frame(0)
    send_mod.wait_recv()
    norm_chunk(frame0, mod_next, 0)
    for copy in load_kv:
        copy.wait()
    kv_copies = []
    project_kv(0)
    kv_copies.append(send_kv(0, 0))
    for c in range(1, chunks):
        wait_frame(c)
        norm_chunk(frame0, mod_next, c)
        project_kv(c)
        kv_copies.append(send_kv(0, c))
    wo_forward(0)
    load_q.wait()
    project_q(0)
    wo_forward(1)
    for c in range(1, chunks):
        project_q(c)
    exchanged = attention(0, q == last, kv_copies, wo_forward_far)
    wo_other_side()
    wo_finish()
    partials = output_projection(0, exchanged)

    def send_shifted(u):
        c, k = units[u]
        lanes = pl.ds(k * part_cols, part_cols)
        partials[u].wait_recv()
        z_send[c, :, lanes] = new_state(frame0, mod_next, 0, c, k)
        place = frame1.at[c, block(t), lanes]
        to = dev(queue_at(2), partner)
        copy = remote(z_send.at[c, :, lanes], place, to)
        counter[0] -= 1
        entering = remote(noise.at[1, pl.ds(c * rows, rows), lanes], place, to, keep=False)

        @pl.when(q == last - 1)
        def _():
            entering.start()

        @pl.when(q != last - 1)
        def _():
            copy.start()

        return copy

    n_units = len(units)
    shifted = [None] * n_units
    cut = CUT if part_cols == CUT_PART else part_cols // 2
    gathers = [Gather(frame1, c, k, 1 - y, part_cols) for c, k in units]

    def first_after_shift(u):
        shifted[u].wait_recv()
        gathers[u].first()

    for tick in range(n_units + 3):
        if tick < n_units:
            shifted[tick] = send_shifted(tick)
        if 0 <= tick - 1 < n_units:
            first_after_shift(tick - 1)
        if 0 <= tick - 2 < n_units:
            gathers[tick - 2].second()
            gathers[tick - 2].forward_own()
        if 0 <= tick - 3 < parts:
            gathers[tick - 3].forward_other()

    for copy in kv_copies:
        copy.wait_send()
    sent[:] = [copy for copy in sent if all(copy is not done for done in kv_copies)]
    kv_copies = []
    for c in range(chunks):
        if c + 1 < chunks and chunks > 2:
            for k in range(parts):
                gathers[(c + 1) * parts + k].forward_other()
        for k in range(parts):
            gathers[c * parts + k].wait()
        norm_chunk(frame1, mod_own, c)
        project_kv(c)
        kv_copies.append(send_kv(1, c))
        if c + 1 < chunks and chunks == 2:
            for k in range(parts):
                gathers[(c + 1) * parts + k].forward_other()
        project_q(c)
    exchanged = attention(1, q == 0, kv_copies)
    partials = output_projection(1, exchanged)
    gathers = [Gather(frame2, c, k, y, cut) for c, k in units]

    for tick in range(n_units + 2):
        if tick < n_units:
            c, k = units[tick]
            partials[tick].wait_recv()
            frame2[c, block(t), pl.ds(k * part_cols, part_cols)] = new_state(
                frame1, mod_own, 1, c, k
            )
            gathers[tick].first()
        if 0 <= tick - 1 < n_units:
            gathers[tick - 1].second()
            gathers[tick - 1].forward_own()
        if 0 <= tick - 2 < n_units:
            gathers[tick - 2].forward_other()
    for gather in gathers:
        gather.wait()
    for copy in sent:
        copy.wait_send()
    for c, k, copy in noise_copies:

        @pl.when(q == noise_from[k, c])
        def _():
            copy.wait_send()


def body(
    latents, levels, mod_table, step_size, qkv_weight, q_gain, k_gain, out_weight, fresh_noise
):
    frame_rows, width = latents.shape[1:]
    cols = qkv_weight.shape[2]
    heads = cols // HD
    n_tensor = lax.axis_size("tensor")
    chunks = CHUNKS
    chunk_rows = frame_rows // chunks
    rows = chunk_rows // n_tensor
    bf16, f32 = jnp.bfloat16, jnp.float32
    frame = pltpu.VMEM((chunks, chunk_rows, width), bf16)
    anywhere = pl.BlockSpec(memory_space=pl.ANY)
    vmem = pl.BlockSpec(memory_space=pltpu.VMEM)
    n_copies = 256
    out = pl.pallas_call(
        kernel,
        out_shape=pltpu.VMEM((chunks, chunk_rows, width), bf16),
        in_specs=[pl.BlockSpec(memory_space=pltpu.SMEM)] + [anywhere] * 4 + [vmem] * 4,
        out_specs=vmem,
        scratch_shapes=[
            frame, frame, frame,
            pltpu.VMEM((width, 2 * cols), bf16),
            pltpu.VMEM((width, cols), bf16),
            pltpu.VMEM((n_tensor // 2 * cols, width), bf16),
            pltpu.VMEM((chunks, chunk_rows, cols), bf16),
            pltpu.VMEM((2, frame_rows, cols), bf16),
            pltpu.VMEM((STEPS, 2, frame_rows, cols), bf16),
            pltpu.VMEM((8, width), f32),
            pltpu.VMEM((8, width), f32),
            pltpu.VMEM((8, HD), f32),
            pltpu.VMEM((chunks, chunk_rows, cols), f32),
            pltpu.VMEM((chunk_rows, HD), f32),
            pltpu.VMEM((chunks, heads, chunk_rows, HD), f32),
            pltpu.VMEM((chunks, heads, chunk_rows, HD), f32),
            pltpu.VMEM((STEPS, chunks, chunk_rows, cols), bf16),
            pltpu.VMEM((STEPS, chunks, 2 * rows, n_tensor // 2 * cols), bf16),
            pltpu.VMEM((chunks, rows, width), f32),
            pltpu.VMEM((STEPS, chunks, rows, width), bf16),
            pltpu.VMEM((STEPS, chunks, rows, width), bf16),
            pltpu.VMEM((chunks, rows, width), bf16),
            pltpu.SemaphoreType.DMA((chunks + 4,)),
            pltpu.SemaphoreType.DMA((n_copies,)),
            pltpu.SemaphoreType.DMA((n_copies,)),
        ],
        compiler_params=pltpu.CompilerParams(
            collective_id=0, has_side_effects=True, vmem_limit_bytes=54 * 1024 * 1024
        ),
        name="denoise",
    )(
        levels, latents, fresh_noise, qkv_weight, out_weight, mod_table,
        step_size[None], q_gain[None], k_gain[None],
    )
    out = out.reshape(chunks, n_tensor, rows, width).transpose(1, 0, 2, 3)
    return out.reshape(1, frame_rows, width)


def solution(mesh):
    return jax.shard_map(
        body,
        mesh=mesh,
        in_specs=(
            P("queue", None, None),
            P("queue"),
            P(),
            P(),
            P(None, None, "tensor"),
            P(),
            P(),
            P("tensor", None),
            P(None, "tensor", None),
        ),
        out_specs=P("queue", None, None),
        check_vma=False,
    )
```

```python
import functools
import math

import jax
import jax.numpy as jnp
from jax import lax
from jax.experimental import pallas as pl
from jax.experimental.pallas import tpu as pltpu
from jax.sharding import PartitionSpec as P

HD = 128
STEPS = 2
CHUNKS = 3
PARTS = 2
CUT_PART = 1536
CUT = 1280
MESH = pl.DeviceIdType.MESH
NOISE_FROM = {1: (15, 15), 2: (15, 15), 3: (3, 3), 4: (11, 11), 5: (2, 10), 6: (15, 15), 7: (13, 13)}


def dot(a, b):
    return jnp.dot(a, b, preferred_element_type=jnp.float32)


def kernel(
    levels, lat, noise, wqkv, wout, mod_table, step_size, q_gain, k_gain, frame2,
    frame0, frame1, normed, wkv, wq, wo, q_buf, kv, kv_prev, mod_own, mod_next, gains,
    acc, lowest, top, total, att, att_all, own_part, part_send, part_recv, z_send,
    load_sem, send_sem, recv_sem,
):
    n_queue, n_tensor = lax.axis_size("queue"), lax.axis_size("tensor")
    n_x = n_tensor // 2
    q, t = lax.axis_index("queue"), lax.axis_index("tensor")
    x, y = t // 2, t % 2
    core = q % 2
    chunks, chunk_rows, width = frame0.shape
    rows = chunk_rows // n_tensor
    cols = wq.shape[1]
    heads = cols // HD
    half = width // 2
    last = n_queue - 1
    noise_from = {
        (k, c): (v[c % 2] if v[c % 2] <= last else last)
        for k, v in NOISE_FROM.items()
        for c in range(chunks)
    }

    def dev(queue=None, tensor=None):
        return {"queue": q if queue is None else queue, "tensor": t if tensor is None else tensor}

    def tensor_of(xx, yy):
        return lax.rem(xx + n_x, n_x) * 2 + yy

    def queue_at(d):
        return lax.rem(q + d + n_queue, n_queue)

    counter = [0]
    sent = []

    def remote(src, dst, to, keep=True):
        i = counter[0]
        counter[0] += 1
        copy = pltpu.make_async_remote_copy(
            src_ref=src, dst_ref=dst, send_sem=send_sem.at[i], recv_sem=recv_sem.at[i],
            device_id=to, device_id_type=MESH,
        )
        if keep:
            sent.append(copy)
        return copy

    def block(owner):
        return pl.ds(pl.multiple_of(owner * rows, 16), rows)

    barrier = pltpu.get_barrier_semaphore()
    partners = [dev(tensor=jnp.bitwise_xor(t, k)) for k in range(1, n_tensor)]
    near = {1, n_queue - 1} | ({4, n_queue - 4} if n_queue > 4 else set())
    partners += [dev(queue=queue_at(d)) for d in sorted(near)]
    partners += [dev(queue_at(d), jnp.bitwise_xor(t, 1)) for d in sorted({2, n_queue - 2})]
    for to in partners:
        pl.semaphore_signal(barrier, inc=1, device_id=to, device_id_type=MESH)
    extra = sorted({(k, v) for (k, _), v in noise_from.items() if v != last})
    for k, v in extra:

        @pl.when(q == v)
        def _():
            pl.semaphore_signal(
                barrier, inc=1, device_id=dev(last, jnp.bitwise_xor(t, k)), device_id_type=MESH
            )

        @pl.when(q == last)
        def _():
            pl.semaphore_signal(
                barrier, inc=1, device_id=dev(v, jnp.bitwise_xor(t, k)), device_id_type=MESH
            )

    def load(src, dst, i):
        return pltpu.make_async_copy(src, dst, load_sem.at[i])

    def lat_rows(ref, owner, c):
        return ref.at[0, pl.ds(owner * rows * chunks + c * rows, rows), :]

    own_noise = [
        load(noise.at[0, pl.ds(c * rows, rows), :], frame0.at[c, block(t), :], c)
        for c in range(chunks)
    ]

    @pl.when(q != last)
    def _():
        for owner in range(n_tensor):
            load(lat_rows(lat, owner, 0), frame0.at[0, pl.ds(owner * rows, rows), :], 0).start()

    @pl.when(q == last)
    def _():
        for c in range(chunks):
            own_noise[c].start()

    load_kv = [load(wqkv.at[j + 1], wkv.at[:, pl.ds(j * cols, cols)], chunks + j) for j in range(2)]
    load_q = load(wqkv.at[0], wq, chunks + 2)
    own_wo = pl.ds(pl.multiple_of(x * cols, HD), cols)
    load_o = load(wout, wo.at[own_wo, :], chunks + 3)
    for copy in load_kv:
        copy.start()

    @pl.when(q != last)
    def _():
        for c in range(1, chunks):
            for owner in range(n_tensor):
                load(lat_rows(lat, owner, c), frame0.at[c, pl.ds(owner * rows, rows), :], c).start()

    load_q.start()
    load_o.start()

    n_levels = mod_table.shape[0]
    hot = lax.broadcasted_iota(jnp.int32, (8, n_levels), 1) == levels[0]
    rate = jnp.sum(jnp.where(hot, step_size[...], 0.0), axis=1, keepdims=True)[0:1]
    hot = hot.astype(jnp.float32).astype(jnp.bfloat16)
    mod_own[...] = jnp.zeros_like(mod_own)
    lowest[...] = jnp.full(lowest.shape, -3e38, jnp.float32)
    mod_own[0:1, :] = dot(hot, mod_table[:, :width])[0:1]
    mod_own[1:2, :] = 1.0 + dot(hot, mod_table[:, width : 2 * width])[0:1]
    mod_own[2:3, :] = rate * dot(hot, mod_table[:, 2 * width :])[0:1]
    gains[0:1, :] = q_gain[...] * (math.log2(math.e) / math.sqrt(HD))
    gains[1:2, :] = k_gain[...]

    arrivals = len(partners)
    for _, v in extra:
        arrivals = arrivals + (q == v).astype(jnp.int32) + (q == last).astype(jnp.int32)
    pl.semaphore_wait(barrier, arrivals)

    send_mod = remote(mod_own, mod_next, dev(queue=queue_at(-1)))
    send_mod.start()
    noise_copies = []
    for c in range(chunks):
        for k in range(1, n_tensor):
            copy = remote(
                noise.at[0, pl.ds(c * rows, rows), :], frame0.at[c, block(t), :],
                dev(last, jnp.bitwise_xor(t, k)), keep=False,
            )
            noise_copies.append((c, k, copy))

            @pl.when(q == noise_from[k, c])
            def _():
                copy.start()

    n_z = n_queue // 4
    z_side = (q // 4) % 2 if n_z > 1 else 0
    sides = 2 if n_z > 1 else 1
    share = width // (2 * sides)

    def share_cols(side, part=None):
        start = (side * 2 + core) * share
        if part is None:
            return pl.ds(pl.multiple_of(start, HD), share)
        return pl.ds(pl.multiple_of(start + part * (share // 2), HD), share // 2)

    def wo_region(xx, side, part=None, row_part=None):
        start, size = lax.rem(xx + n_x, n_x) * cols, cols
        if row_part is not None:
            start, size = start + row_part * (cols // 2), cols // 2
        return wo.at[pl.ds(pl.multiple_of(start, 16), size), share_cols(side, part)]

    other_core = q + 1 - 2 * core
    z_ways = (4, -4)
    wo_direct, wo_far, wo_pass, wo_z = [], [], [], []

    def wo_move(region, to, into):
        copy = remote(region, region, to)
        copy.start()
        into.append(copy)

    def wo_start():
        for e in range(2):
            row_half = pl.ds(e * (cols // 2), cols // 2)
            for d in (1, -1):
                copy = remote(
                    wout.at[row_half, share_cols(z_side)], wo_region(x, z_side, row_part=e),
                    dev(tensor=tensor_of(x + d, y)),
                )
                copy.start()
                wo_direct.append(copy)

    def wo_forward(e):
        for i, d in enumerate((1, -1)):
            wo_direct[2 * e + i].wait_recv()
            wo_move(
                wo_region(x - d, z_side, part=i, row_part=e), dev(tensor=tensor_of(x + d, y)), wo_far
            )
            region = wo_region(x - d, z_side, row_part=e)
            if sides == 2:
                wo_move(region, dev(queue=queue_at(z_ways[(i + e) % 2])), wo_z)
            wo_move(region, dev(queue=other_core), wo_pass)

    def wo_forward_far():
        for i in range(2):
            for e in range(2):
                wo_far[2 * e + i].wait_recv()
            if sides == 2:
                wo_move(wo_region(x + 2, z_side, part=i), dev(queue=queue_at(z_ways[i])), wo_z)
        wo_move(wo_region(x + 2, z_side), dev(queue=other_core), wo_pass)

    def wo_other_side():
        for copy in wo_z:
            copy.wait_recv()
        if sides == 2:
            for xx in (x - 1, x + 1, x + 2):
                wo_move(wo_region(xx, 1 - z_side), dev(queue=other_core), wo_pass)

    def wo_finish():
        for copy in wo_pass:
            copy.wait_recv()
        load_o.wait()

    def norm_chunk(frame, mod, c):
        tile = chunk_rows // 2

        def step(i, _):
            at = pl.ds(pl.multiple_of(i * tile, 16), tile)
            state = frame[c, at, :].astype(jnp.float32)
            scale = lax.rsqrt(jnp.mean(state * state, axis=-1, keepdims=True) + 1e-06)
            normed[c, at, :] = (state * scale * mod[1:2, :] + mod[0:1, :]).astype(jnp.bfloat16)
            return 0

        lax.fori_loop(0, chunk_rows // tile, step, 0)

    def head_norm(part, gain):
        scale = lax.rsqrt(jnp.mean(part * part, axis=-1, keepdims=True) + 1e-06)
        return (part * scale * gain).astype(jnp.bfloat16)

    def project_kv(c):
        at = pl.ds(c * chunk_rows, chunk_rows)
        both = dot(normed[c], wkv[...])
        for h in range(heads):
            lanes = slice(h * HD, (h + 1) * HD)
            kv[0, at, lanes] = head_norm(both[:, lanes], gains[1:2, :])
        kv[1, at, :] = both[:, cols:].astype(jnp.bfloat16)

    def project_q(c):
        part = dot(normed[c], wq[...])
        for h in range(heads):
            lanes = slice(h * HD, (h + 1) * HD)
            q_buf[c, :, lanes] = head_norm(part[:, lanes], gains[0:1, :])

    def send_kv(step, c):
        at = pl.ds(c * chunk_rows, chunk_rows)
        copy = remote(kv.at[:, at, :], kv_prev.at[step, :, at, :], dev(queue=queue_at(1)))
        copy.start()
        return copy

    def attend(c, h, keys, values, before):
        lanes = slice(h * HD, (h + 1) * HD)
        logits = lax.dot_general(
            q_buf[c, :, lanes], keys[:, lanes], (((1,), (1,)), ((), ())),
            preferred_element_type=jnp.float32,
        )
        peak = jnp.max(logits, axis=-1, keepdims=True)
        peak = jnp.maximum(before, jnp.broadcast_to(peak, (chunk_rows, HD)))
        tiled = jnp.concatenate([peak] * (logits.shape[1] // HD), axis=1)
        raised = jnp.exp2(logits - tiled).astype(jnp.bfloat16)
        ones = jnp.ones((values.shape[0], HD), jnp.bfloat16)
        both = dot(raised, jnp.concatenate([values[:, lanes], ones], axis=1))
        return both[:, :HD], both[:, HD:], peak

    def attend_own(c):
        for h in range(heads):
            summed, weight, peak = attend(c, h, kv.at[0], kv.at[1], lowest[...])
            acc[c, :, h * HD : (h + 1) * HD] = summed
            total[c, h] = weight
            top[c, h] = peak

    def attend_prev(step, c):
        for h in range(heads):
            lanes = slice(h * HD, (h + 1) * HD)
            before = top[c, h]
            summed, weight, peak = attend(
                c, h, kv_prev.at[step, 0], kv_prev.at[step, 1], before
            )
            fade = jnp.exp2(before - peak)
            weight = total[c, h] * fade + weight
            summed = acc[c, :, lanes] * fade + summed
            att[step, c, :, lanes] = (summed / weight).astype(jnp.bfloat16)

    def attend_alone(step, c):
        for h in range(heads):
            lanes = slice(h * HD, (h + 1) * HD)
            att[step, c, :, lanes] = (acc[c, :, lanes] / total[c, h]).astype(jnp.bfloat16)

    def exchange_att(step, c):
        mine = pl.ds(pl.multiple_of(x * cols, HD), cols)
        copies = []
        for d in range(1, n_x):
            xx = lax.rem(x + d, n_x)
            at = pl.ds(pl.multiple_of(xx * 2 * rows, 16), 2 * rows)
            copy = remote(
                att.at[step, c, at, :], att_all.at[step, c, :, mine],
                dev(tensor=tensor_of(xx, y)),
            )
            copy.start()
            copies.append(copy)
        at = pl.ds(pl.multiple_of(x * 2 * rows, 16), 2 * rows)
        att_all[step, c, :, mine] = att[step, c, at, :]
        return copies

    parts = PARTS
    part_cols = width // parts
    units = [(c, k) for c in range(chunks) for k in range(parts)]

    def project_out(step, c, k):
        lanes = pl.ds(k * part_cols, part_cols)
        part = dot(att_all[step, c], wo[:, lanes])
        low, high = part[:rows], part[rows:]
        own_part[c, :, lanes] = jnp.where(y == 0, low, high)
        part_send[step, c, :, lanes] = jnp.where(y == 0, high, low).astype(jnp.bfloat16)
        copy = remote(
            part_send.at[step, c, :, lanes], part_recv.at[step, c, :, lanes], dev(tensor=partner)
        )
        copy.start()
        return copy

    def new_state(frame, mod, step, c, k):
        lanes = pl.ds(k * part_cols, part_cols)
        update = own_part[c, :, lanes] + part_recv[step, c, :, lanes].astype(jnp.float32)
        state = frame[c, block(t), lanes].astype(jnp.float32)
        return (state + mod[2:3, lanes] * update).astype(jnp.bfloat16)

    def move(frame, c, owner, lanes, to):
        region = frame.at[c, block(owner), lanes]
        copy = remote(region, region, to)
        copy.start()
        return copy

    partner = jnp.bitwise_xor(t, 1)
    WAYS = (1, -1)

    class Gather:
        def __init__(self, frame, c, k, side, cut):
            self.frame, self.c, self.side = frame, c, side
            self.start = k * part_cols
            self.cut = cut

        def cols(self, low, high):
            return pl.ds(self.start + low, high - low)

        def ring(self, owner_x, side, d, low, high):
            owner = tensor_of(owner_x, side)
            return move(self.frame, self.c, owner, self.cols(low, high), dev(tensor=tensor_of(x + d, y)))

        def cross(self, owner_x, low):
            owner = tensor_of(owner_x, self.side)
            return move(self.frame, self.c, owner, self.cols(low, part_cols), dev(tensor=partner))

        def first(self):
            self.across = self.cross(x, 0)
            self.own = [self.ring(x, self.side, d, 0, part_cols) for d in WAYS]

        def second(self):
            self.across.wait_recv()
            self.other = [self.ring(x, 1 - self.side, d, 0, self.cut) for d in WAYS]

        def forward_own(self):
            mid = part_cols // 2
            self.far, self.crossed = [], []
            for copy, d in zip(self.own, WAYS):
                copy.wait_recv()
                low, high = (0, mid) if d == 1 else (mid, part_cols)
                self.far.append(self.ring(x - d, self.side, d, low, high))
                if self.cut < part_cols:
                    self.crossed.append(self.cross(x - d, self.cut))

        def forward_other(self):
            mid = self.cut // 2
            self.far_other = []
            for copy, d in zip(self.other, WAYS):
                copy.wait_recv()
                low, high = (0, mid) if d == 1 else (mid, self.cut)
                self.far_other.append(self.ring(x - d, 1 - self.side, d, low, high))
            if self.cut < part_cols:
                self.far[1].wait_recv()
                self.crossed.append(self.cross(x + 2, self.cut))

        def wait(self):
            self.far[0].wait_recv()
            if self.cut == part_cols:
                self.far[1].wait_recv()
            for copy in self.far_other + self.crossed:
                copy.wait_recv()

    def output_projection(step, exchanged):
        partials = []
        for c in range(chunks):
            for copy in exchanged[c]:
                copy.wait_recv()
            for k in range(parts):
                partials.append(project_out(step, c, k))
        return partials

    def attention(step, position_zero, kv_copies, between=None):
        for c in range(chunks):
            attend_own(c)
            if between is not None and c == 0:
                between()
        for copy in kv_copies:
            copy.wait_recv()
        exchanged = []
        for c in range(chunks):

            @pl.when(position_zero)
            def _():
                attend_alone(step, c)

            @pl.when(jnp.logical_not(position_zero))
            def _():
                attend_prev(step, c)

            exchanged.append(exchange_att(step, c))
        return exchanged

    def wait_frame(c):
        @pl.when(q != last)
        def _():
            pltpu.make_async_copy(frame0.at[c], frame0.at[c], load_sem.at[c]).wait()

        @pl.when(q == last)
        def _():
            own_noise[c].wait()
            for cc, k, copy in noise_copies:
                if cc == c:
                    copy.wait_recv()

    wo_start()
    wait_frame(0)
    send_mod.wait_recv()
    norm_chunk(frame0, mod_next, 0)
    for copy in load_kv:
        copy.wait()
    kv_copies = []
    project_kv(0)
    kv_copies.append(send_kv(0, 0))
    for c in range(1, chunks):
        wait_frame(c)
        norm_chunk(frame0, mod_next, c)
        project_kv(c)
        kv_copies.append(send_kv(0, c))
    wo_forward(0)
    load_q.wait()
    project_q(0)
    wo_forward(1)
    for c in range(1, chunks):
        project_q(c)
    exchanged = attention(0, q == last, kv_copies, wo_forward_far)
    wo_other_side()
    wo_finish()
    partials = output_projection(0, exchanged)

    def send_shifted(u):
        c, k = units[u]
        lanes = pl.ds(k * part_cols, part_cols)
        partials[u].wait_recv()
        z_send[c, :, lanes] = new_state(frame0, mod_next, 0, c, k)
        place = frame1.at[c, block(t), lanes]
        to = dev(queue_at(2), partner)
        copy = remote(z_send.at[c, :, lanes], place, to)
        counter[0] -= 1
        entering = remote(noise.at[1, pl.ds(c * rows, rows), lanes], place, to, keep=False)

        @pl.when(q == last - 1)
        def _():
            entering.start()

        @pl.when(q != last - 1)
        def _():
            copy.start()

        return copy

    n_units = len(units)
    shifted = [None] * n_units
    cut = CUT if part_cols == CUT_PART else part_cols // 2
    gathers = [Gather(frame1, c, k, 1 - y, cut) for c, k in units]

    def first_after_shift(u):
        shifted[u].wait_recv()
        gathers[u].first()

    for tick in range(n_units + 3):
        if tick < n_units:
            shifted[tick] = send_shifted(tick)
        if 0 <= tick - 1 < n_units:
            first_after_shift(tick - 1)
        if 0 <= tick - 2 < n_units:
            gathers[tick - 2].second()
            gathers[tick - 2].forward_own()
        if 0 <= tick - 3 < parts:
            gathers[tick - 3].forward_other()

    for copy in kv_copies:
        copy.wait_send()
    sent[:] = [copy for copy in sent if all(copy is not done for done in kv_copies)]
    kv_copies = []
    for c in range(chunks):
        if c + 1 < chunks and chunks > 2:
            for k in range(parts):
                gathers[(c + 1) * parts + k].forward_other()
        for k in range(parts):
            gathers[c * parts + k].wait()
        norm_chunk(frame1, mod_own, c)
        project_kv(c)
        kv_copies.append(send_kv(1, c))
        if c + 1 < chunks and chunks == 2:
            for k in range(parts):
                gathers[(c + 1) * parts + k].forward_other()
        project_q(c)
    exchanged = attention(1, q == 0, kv_copies)
    partials = output_projection(1, exchanged)
    gathers = [Gather(frame2, c, k, y, cut) for c, k in units]

    for tick in range(n_units + 2):
        if tick < n_units:
            c, k = units[tick]
            partials[tick].wait_recv()
            frame2[c, block(t), pl.ds(k * part_cols, part_cols)] = new_state(
                frame1, mod_own, 1, c, k
            )
            gathers[tick].first()
        if 0 <= tick - 1 < n_units:
            gathers[tick - 1].second()
            gathers[tick - 1].forward_own()
        if 0 <= tick - 2 < n_units:
            gathers[tick - 2].forward_other()
    for gather in gathers:
        gather.wait()
    for copy in sent:
        copy.wait_send()
    for c, k, copy in noise_copies:

        @pl.when(q == noise_from[k, c])
        def _():
            copy.wait_send()


def body(
    latents, levels, mod_table, step_size, qkv_weight, q_gain, k_gain, out_weight, fresh_noise
):
    frame_rows, width = latents.shape[1:]
    cols = qkv_weight.shape[2]
    heads = cols // HD
    n_tensor = lax.axis_size("tensor")
    chunks = CHUNKS
    chunk_rows = frame_rows // chunks
    rows = chunk_rows // n_tensor
    bf16, f32 = jnp.bfloat16, jnp.float32
    frame = pltpu.VMEM((chunks, chunk_rows, width), bf16)
    anywhere = pl.BlockSpec(memory_space=pl.ANY)
    vmem = pl.BlockSpec(memory_space=pltpu.VMEM)
    n_copies = 320
    out = pl.pallas_call(
        kernel,
        out_shape=pltpu.VMEM((chunks, chunk_rows, width), bf16),
        in_specs=[pl.BlockSpec(memory_space=pltpu.SMEM)] + [anywhere] * 4 + [vmem] * 4,
        out_specs=vmem,
        scratch_shapes=[
            frame, frame, frame,
            pltpu.VMEM((width, 2 * cols), bf16),
            pltpu.VMEM((width, cols), bf16),
            pltpu.VMEM((n_tensor // 2 * cols, width), bf16),
            pltpu.VMEM((chunks, chunk_rows, cols), bf16),
            pltpu.VMEM((2, frame_rows, cols), bf16),
            pltpu.VMEM((STEPS, 2, frame_rows, cols), bf16),
            pltpu.VMEM((8, width), f32),
            pltpu.VMEM((8, width), f32),
            pltpu.VMEM((8, HD), f32),
            pltpu.VMEM((chunks, chunk_rows, cols), f32),
            pltpu.VMEM((chunk_rows, HD), f32),
            pltpu.VMEM((chunks, heads, chunk_rows, HD), f32),
            pltpu.VMEM((chunks, heads, chunk_rows, HD), f32),
            pltpu.VMEM((STEPS, chunks, chunk_rows, cols), bf16),
            pltpu.VMEM((STEPS, chunks, 2 * rows, n_tensor // 2 * cols), bf16),
            pltpu.VMEM((chunks, rows, width), f32),
            pltpu.VMEM((STEPS, chunks, rows, width), bf16),
            pltpu.VMEM((STEPS, chunks, rows, width), bf16),
            pltpu.VMEM((chunks, rows, width), bf16),
            pltpu.SemaphoreType.DMA((chunks + 4,)),
            pltpu.SemaphoreType.DMA((n_copies,)),
            pltpu.SemaphoreType.DMA((n_copies,)),
        ],
        compiler_params=pltpu.CompilerParams(
            collective_id=0, has_side_effects=True, vmem_limit_bytes=54 * 1024 * 1024
        ),
        name="denoise",
    )(
        levels, latents, fresh_noise, qkv_weight, out_weight, mod_table,
        step_size[None], q_gain[None], k_gain[None],
    )
    out = out.reshape(chunks, n_tensor, rows, width).transpose(1, 0, 2, 3)
    return out.reshape(1, frame_rows, width)


def solution(mesh):
    return jax.shard_map(
        body,
        mesh=mesh,
        in_specs=(
            P("queue", None, None),
            P("queue"),
            P(),
            P(),
            P(None, None, "tensor"),
            P(),
            P(),
            P("tensor", None),
            P(None, "tensor", None),
        ),
        out_specs=P("queue", None, None),
        check_vma=False,
    )
```
